256 devices in a mesh: req: 128 (over y, z, x), patch: 2 (over core).
Axes of the slice: x: 4, y: 4, z: 8, core: 2. Of those that a mesh axis runs over, the one named last changes fastest.
Arguments:
- latents: bfloat16 [128, 8, 128, 640], P('req', 'patch'), may hold values from -6 to 6
- previous_key_values: bfloat16 [128, 1024, 1280], P('req', 'patch'), may hold values from -6 to 6
- convolution_kernel_weight: bfloat16 [5760, 640], replicated, may hold values from -0.078125 to 0.078125
- layer_norm_gain: float32 [640], replicated, may hold values from 0.25 to 1.75
- query_matrix: bfloat16 [640, 640], replicated, may hold values from -0.237170825 to 0.237170825
- key_matrix: bfloat16 [640, 640], replicated, may hold values from -10.751744 to 10.751744
- value_matrix: bfloat16 [640, 640], replicated, may hold values from -0.25 to 0.25
- output_matrix: bfloat16 [640, 640], replicated, may hold values from -0.25 to 0.25
- adapter_table: bfloat16 [128, 573440], P('req'), may hold values from -0.14941406 to 0.14941406
- request_adapter_choice: int32 [128], replicated, may hold values from 0 to 127
- parent_request: int32 [128], replicated, may hold values from 0 to 127
- adapter_bank_row: int32 [128], replicated, may hold values from 0 to 127, each once
Outputs:
- block_out: bfloat16 [128, 8, 128, 640], P('req', 'patch')
The draws below stay inside these ranges and needn't reach their ends.
Inputs may be any that keep to these rules, and one draw needn't show every extreme that they name: `adapter_bank_row`: each bank row appears once.
All inputs are finite; a program needn't handle non-finite values.
Results may differ from the reference program's by a relative error of at most 0.0075.
Values may be sent and summed in bfloat16 or wider, within the bound.
A program may use at most 128 MiB of HBM per device.

```python
import math
import jax
import jax.numpy as jnp
import numpy as np
from jax import lax

HEADS = 10
CHANNEL_COUNT = 640
ADAPTER_RANK = 64
W = 128
H_DEV = 4
PARTICLES = 128
ADAPTER_COUNT = 128
ADAPTER_ENTRIES = 573440


def shared_query(key):
    base = jax.random.normal(key, (CHANNEL_COUNT, CHANNEL_COUNT), jnp.float32)
    return jnp.clip(base, -6.0, 6.0) * CHANNEL_COUNT ** (-0.5)


def draw_query_matrix(key, part):
    base = shared_query(key)
    return base.astype(jnp.bfloat16)


def draw_key_matrix(key, part):
    key = jax.random.fold_in(key, 12)
    noise = jnp.clip(jax.random.normal(key, (CHANNEL_COUNT, CHANNEL_COUNT), jnp.float32), -6.0, 6.0) * CHANNEL_COUNT ** (-0.5)
    return noise.astype(jnp.bfloat16)


def with_ends(values, own_key, smallest, largest):
    longest = values.shape.index(max(values.shape))
    spots = []
    for shift in (0, 1):
        where = [jax.random.randint(jax.random.fold_in(own_key, axis), (), 0, length) for axis, length in enumerate(values.shape)]
        where[longest] = (where[longest] + shift) % values.shape[longest]
        spots.append(tuple(where))
    return values.at[spots[0]].set(smallest).at[spots[1]].set(largest)


def level_of(own_key, extent, shards, low, top_value):
    level = 1.0
    for axis_at, blocks in shards:
        steps = jax.random.uniform(jax.random.fold_in(jax.random.fold_in(own_key, 6), axis_at), (blocks,), jnp.float32, low / len(shards), top_value / len(shards))
        level = level * jnp.repeat(jnp.exp(steps), extent[axis_at] // blocks).reshape((-1,) + (1,) * (len(extent) - 1 - axis_at))
    return level


def rank_table(amount, slope):
    portions = [(1 << 20) // math.isqrt(standing ** slope) + 1 for standing in range(1, amount + 1)]
    scale = 1 + sum(portions) // (1 << 30)
    return np.cumsum(np.array([max(1, weight // scale) for weight in portions]))


def skewed_ids(key, shape, number_of, slope):
    grid = rank_table(number_of, slope)
    ticket = jax.random.randint(jax.random.fold_in(key, 1), shape, 0, int(grid[number_of - 1]))
    grade = jnp.searchsorted(jnp.asarray(grid, jnp.int32), ticket, side="right")
    return jax.random.permutation(jax.random.fold_in(key, 2), number_of)[grade].astype(jnp.int32)


def centred(rng, shape, width, reach, cuts=(), kind=jnp.bfloat16):
    gain = level_of(rng, shape, cuts, -0.22, 0.18) if cuts else 1.0
    array = jax.random.normal(rng, shape, jnp.float32) * width * gain
    return jnp.minimum(jnp.maximum(array, -reach), reach).astype(kind)


def setup_inputs(seed: int = 0) -> dict:
    key_of = jax.random.split(jax.random.key(seed), 13)
    return {
        "latents": centred(key_of[0], (PARTICLES, 2 * H_DEV, W, CHANNEL_COUNT), 1.0, 6.0, ((0, 128), (1, 2))),
        "previous_key_values": centred(key_of[1], (PARTICLES, 2 * H_DEV * W, 2 * CHANNEL_COUNT), 1.0, 6.0, ((0, 128), (1, 2))),
        "convolution_kernel_weight": centred(key_of[2], (9 * CHANNEL_COUNT, CHANNEL_COUNT), (9 * CHANNEL_COUNT) ** -0.5, 0.078125),
        "layer_norm_gain": jnp.clip(1.0 + 0.15 * jax.random.normal(key_of[3], (CHANNEL_COUNT,), jnp.float32), 0.25, 1.75),
        "query_matrix": draw_query_matrix(jax.random.fold_in(key_of[12], 71), 0),
        "key_matrix": draw_key_matrix(jax.random.fold_in(key_of[12], 71), 0),
        "value_matrix": centred(key_of[6], (CHANNEL_COUNT, CHANNEL_COUNT), CHANNEL_COUNT ** -0.5, 0.25),
        "output_matrix": centred(key_of[7], (CHANNEL_COUNT, CHANNEL_COUNT), CHANNEL_COUNT ** -0.5, 0.25),
        "adapter_table": centred(key_of[8], (ADAPTER_COUNT, ADAPTER_ENTRIES), 0.025, 0.14941406, ((0, 128),)),
        "request_adapter_choice": with_ends(skewed_ids(key_of[9], (PARTICLES,), ADAPTER_COUNT, 2), jax.random.fold_in(key_of[9], 3), 0, ADAPTER_COUNT - 1).astype(jnp.int32),
        "parent_request": with_ends(skewed_ids(key_of[10], (PARTICLES,), PARTICLES, 2), jax.random.fold_in(key_of[10], 3), 0, PARTICLES - 1).astype(jnp.int32),
        "adapter_bank_row": jax.random.permutation(key_of[11], ADAPTER_COUNT).astype(jnp.int32),
    }


def keep_bf(value):
    return lax.optimization_barrier(value.astype(jnp.bfloat16))

def split_adapter_vector(flat_vector, piece_width, adapter_rank_value):
    sizes = [9 * piece_width * adapter_rank_value, adapter_rank_value * piece_width, piece_width * adapter_rank_value, adapter_rank_value * piece_width, piece_width * adapter_rank_value, adapter_rank_value * piece_width]
    shapes = [(9 * piece_width, adapter_rank_value), (adapter_rank_value, piece_width), (piece_width, adapter_rank_value), (adapter_rank_value, piece_width), (piece_width, adapter_rank_value), (adapter_rank_value, piece_width)]
    adapter_pieces = []
    offset = 0
    for count, piece_shape in zip(sizes, shapes):
        adapter_pieces.append(flat_vector[offset:offset + count].reshape(piece_shape))
        offset = offset + count
    return adapter_pieces

def conv_columns(act):
    rows, cols, piece_width = act.shape
    padded = jnp.pad(act, ((1, 1), (1, 1), (0, 0)))
    taps = [padded[dy:dy + rows, dx:dx + cols] for dy in range(3) for dx in range(3)]
    return jnp.stack(taps, axis=2).reshape(rows * cols, 9 * piece_width)

def attend(query, keys, values, heads):
    count, piece_width = query.shape
    depth = piece_width // heads
    q3 = query.astype(jnp.float32).reshape(count, heads, depth)
    k3 = keys.astype(jnp.float32).reshape(keys.shape[0], heads, depth)
    v3 = values.astype(jnp.float32).reshape(keys.shape[0], heads, depth)
    scores = jnp.einsum('qhd,khd->hqk', q3, k3) / jnp.sqrt(jnp.float32(depth))
    scores = scores - lax.optimization_barrier(jnp.max(scores, axis=-1, keepdims=True))
    weights = jnp.exp(scores)
    probs = keep_bf(weights / lax.optimization_barrier(jnp.sum(weights, axis=-1, keepdims=True))).astype(jnp.float32)
    mixed = jnp.einsum('hqk,khd->qhd', probs, v3)
    return mixed.reshape(count, piece_width).astype(jnp.bfloat16)

def reference(latents, previous_key_values, convolution_kernel_weight, layer_norm_gain, query_matrix, key_matrix, value_matrix, output_matrix, adapter_table, request_adapter_choice, parent_request, adapter_bank_row):
    rows_of = adapter_bank_row[request_adapter_choice[parent_request]].astype(jnp.int32)

    def particle(inputs):
        band, stale, bank_row_index = inputs
        adapter_vector = lax.dynamic_index_in_dim(adapter_table, bank_row_index, 0, keepdims=False)
        convolution_down_matrix, convolution_up_matrix, query_down_matrix, query_up_matrix, value_down_matrix, value_up_matrix = split_adapter_vector(adapter_vector, CHANNEL_COUNT, ADAPTER_RANK)
        act = jax.nn.silu(band.astype(jnp.float32)).astype(jnp.bfloat16)
        cols = conv_columns(act)
        low = jnp.dot(cols, convolution_down_matrix, preferred_element_type=jnp.float32).astype(jnp.bfloat16)
        total = band.reshape(-1, CHANNEL_COUNT).astype(jnp.float32) + jnp.dot(cols, convolution_kernel_weight, preferred_element_type=jnp.float32)
        hidden = (total + jnp.dot(low, convolution_up_matrix, preferred_element_type=jnp.float32)).astype(jnp.bfloat16)
        hidden_f = hidden.astype(jnp.float32)
        mean = lax.optimization_barrier(jnp.mean(hidden_f, axis=-1, keepdims=True))
        var = lax.optimization_barrier(jnp.mean((hidden_f - mean) ** 2, axis=-1, keepdims=True))
        normed = (layer_norm_gain * (hidden_f - mean) / jnp.sqrt(var + 1e-05)).astype(jnp.bfloat16)
        query_low = jnp.dot(normed, query_down_matrix, preferred_element_type=jnp.float32).astype(jnp.bfloat16)
        value_low = jnp.dot(normed, value_down_matrix, preferred_element_type=jnp.float32).astype(jnp.bfloat16)
        query = (jnp.dot(normed, query_matrix, preferred_element_type=jnp.float32) + jnp.dot(query_low, query_up_matrix, preferred_element_type=jnp.float32)).astype(jnp.bfloat16)
        keys = jnp.dot(normed, key_matrix, preferred_element_type=jnp.float32).astype(jnp.bfloat16)
        values = (jnp.dot(normed, value_matrix, preferred_element_type=jnp.float32) + jnp.dot(value_low, value_up_matrix, preferred_element_type=jnp.float32)).astype(jnp.bfloat16)
        half = H_DEV * W
        outs = []
        for side in range(2):
            other = 1 - side
            own = slice(side * half, (side + 1) * half)
            far = stale[other * half:(other + 1) * half]
            all_keys = jnp.concatenate([keys[own], far[:, :CHANNEL_COUNT]], axis=0)
            all_values = jnp.concatenate([values[own], far[:, CHANNEL_COUNT:]], axis=0)
            mixed = attend(query[own], all_keys, all_values, HEADS)
            result = hidden[own].astype(jnp.float32) + jnp.dot(mixed, output_matrix, preferred_element_type=jnp.float32)
            outs.append(result.astype(jnp.bfloat16))
        return jnp.concatenate(outs, axis=0).reshape(2 * H_DEV, W, CHANNEL_COUNT)
    return lax.map(particle, (latents, previous_key_values, rows_of))
```

```python
import math
import jax
import jax.numpy as jnp
from jax import lax
from jax.experimental import pallas as pl
from jax.experimental.pallas import tpu as pltpu
from jax.sharding import PartitionSpec as P

MESH = pl.DeviceIdType.MESH
CHIPS = 128
TILES = 140
EXTRA = TILES - CHIPS

def comm_kernel(choice, parent, bank, table, kv, lat, adapter, stale, halo,
                source, spread, spread_extra, picked, picked_extra,
                link_sem, send_sem, recv_sem, extra_sem):
    me = lax.axis_index("req")
    core = lax.axis_index("patch")
    base = core * TILES
    barrier = pltpu.get_barrier_semaphore()
    pl.semaphore_signal(barrier, inc=1, device_id={"patch": 1 - core}, device_id_type=MESH)
    @pl.loop(1, CHIPS)
    def _(k):
        pl.semaphore_signal(barrier, inc=1, device_id={"req": lax.rem(me + k, CHIPS)}, device_id_type=MESH)
    @pl.loop(0, TILES)
    def _(t):
        at = pl.multiple_of((base + t) * 2048, 2048)
        source[t] = table[:, pl.ds(at, 2048)].astype(jnp.float32).reshape(16, 128).astype(jnp.bfloat16)
    pl.semaphore_wait(barrier, CHIPS)

    stale_copy = pltpu.make_async_remote_copy(kv, stale, link_sem.at[0], link_sem.at[1],
        device_id={"patch": 1 - core}, device_id_type=MESH)
    halo_copy = pltpu.make_async_remote_copy(lat.at[0, 3 * (1 - core)], halo, link_sem.at[2], link_sem.at[3],
        device_id={"patch": 1 - core}, device_id_type=MESH)

    @pl.loop(1, CHIPS)
    def _(k):
        d = lax.rem(me + k, CHIPS)
        pltpu.make_async_remote_copy(source.at[d], spread.at[me], send_sem.at[0], recv_sem.at[0],
            device_id={"req": d}, device_id_type=MESH).start()
    @pl.loop(0, EXTRA)
    def _(j):
        d = 10 * j + 5 * core
        @pl.when(d != me)
        def _():
            pltpu.make_async_remote_copy(source.at[CHIPS + j], spread_extra.at[me], extra_sem.at[0], extra_sem.at[1],
                device_id={"req": d}, device_id_type=MESH).start()
    halo_copy.start()
    stale_copy.start()
    j_mine = (me - 5 * core) // 10
    holder = jnp.logical_and(lax.rem(me + 10 - 5 * core, 10) == 0, jnp.logical_and(me >= 5 * core, me < 10 * EXTRA + 5 * core))
    spread[me] = source[me]
    @pl.when(holder)
    def _():
        spread_extra[me] = source[CHIPS + j_mine]
    def wait_many(count, sem):
        r = source.at[pl.ds(0, count)]
        pltpu.make_async_copy(r, r, sem).wait()
    wait_many(CHIPS - 1, recv_sem.at[0])
    @pl.loop(0, CHIPS)
    def _(p):
        picked[p] = spread[bank[choice[parent[p]]]]
    @pl.loop(1, CHIPS)
    def _(k):
        d = lax.rem(me + k, CHIPS)
        pltpu.make_async_remote_copy(picked.at[d], adapter.at[base + me], send_sem.at[1], recv_sem.at[1],
            device_id={"req": d}, device_id_type=MESH).start()
    adapter[base + me] = picked[me]
    @pl.when(holder)
    def _():
        wait_many(CHIPS - 1, extra_sem.at[1])
        @pl.loop(0, CHIPS)
        def _(p):
            picked_extra[p] = spread_extra[bank[choice[parent[p]]]]
        @pl.loop(1, CHIPS)
        def _(k):
            d = lax.rem(me + k, CHIPS)
            pltpu.make_async_remote_copy(picked_extra.at[d], adapter.at[base + CHIPS + j_mine], extra_sem.at[2], extra_sem.at[3],
                device_id={"req": d}, device_id_type=MESH).start()
        adapter[base + CHIPS + j_mine] = picked_extra[me]
    wait_many(CHIPS - 1, recv_sem.at[1])
    @pl.when(holder)
    def _():
        wait_many(EXTRA - 1, extra_sem.at[3])
        wait_many(EXTRA - 1, extra_sem.at[0])
        wait_many(CHIPS - 1, extra_sem.at[2])
    @pl.when(jnp.logical_not(holder))
    def _():
        wait_many(EXTRA, extra_sem.at[3])
        wait_many(EXTRA, extra_sem.at[0])
    mine = adapter.at[pl.ds(base, TILES)]
    forward = pltpu.make_async_remote_copy(mine, mine, link_sem.at[4], link_sem.at[5],
        device_id={"patch": 1 - core}, device_id_type=MESH)
    forward.start()
    wait_many(CHIPS - 1, send_sem.at[0])
    wait_many(CHIPS - 1, send_sem.at[1])
    forward.wait()
    halo_copy.wait()
    stale_copy.wait()

ANY = pl.BlockSpec(memory_space=pl.ANY)
VM = pl.BlockSpec(memory_space=pltpu.VMEM)
SM = pl.BlockSpec(memory_space=pltpu.SMEM)
def exchange(choice, parent, bank, table, kv, lat):
    return pl.pallas_call(
        comm_kernel,
        out_shape=(jax.ShapeDtypeStruct((2 * TILES, 16, 128), jnp.bfloat16),
                   jax.ShapeDtypeStruct(kv.shape, jnp.bfloat16),
                   jax.ShapeDtypeStruct((128, 640), jnp.bfloat16)),
        in_specs=[SM, SM, SM, VM, ANY, ANY],
        out_specs=(VM, ANY, ANY),
        scratch_shapes=[
            pltpu.VMEM((TILES, 16, 128), jnp.bfloat16),
            pltpu.VMEM((CHIPS, 16, 128), jnp.bfloat16),
            pltpu.VMEM((CHIPS, 16, 128), jnp.bfloat16),
            pltpu.VMEM((CHIPS, 16, 128), jnp.bfloat16),
            pltpu.VMEM((CHIPS, 16, 128), jnp.bfloat16),
            pltpu.SemaphoreType.DMA((6,)),
            pltpu.SemaphoreType.DMA((2,)),
            pltpu.SemaphoreType.DMA((2,)),
            pltpu.SemaphoreType.DMA((4,)),
        ],
        compiler_params=pltpu.CompilerParams(collective_id=0, has_side_effects=True, vmem_limit_bytes=40 << 20),
    )(choice, parent, bank, table, kv, lat)

F32, BF16 = jnp.float32, jnp.bfloat16
WIDTH, ROWS, CH, RANK, HEADS = 128, 4, 640, 64, 10
POS = ROWS * WIDTH

def mm(a, b):
    return jnp.dot(a, b, preferred_element_type=F32)

def activate(row, window, x, zero):
    act = jax.nn.silu(x.astype(F32)).astype(BF16).astype(F32)
    if zero is not None:
        act = jnp.where(zero, 0.0, act)
    at = lax.broadcasted_iota(jnp.int32, (WIDTH, CH), 0)
    spot = pl.ds(row * WIDTH, WIDTH)
    window[spot, 0:CH] = jnp.where(at == 0, 0.0, pltpu.roll(act, 1, 0)).astype(BF16)
    window[spot, CH:2 * CH] = act.astype(BF16)
    window[spot, 2 * CH:3 * CH] = jnp.where(at == WIDTH - 1, 0.0, pltpu.roll(act, WIDTH - 1, 0)).astype(BF16)

def unfold_down(adapter, first, tiles, wide):
    pairs = adapter[first:first + tiles].reshape(tiles * 16, 128).astype(F32)
    wide[pl.ds(0, tiles * 16, stride=2), :] = pairs
    wide[pl.ds(1, tiles * 16, stride=2), :] = pltpu.roll(pairs, RANK, 1)

def unfold_up(adapter, first, wide):
    wide[0:320, :] = adapter[first:first + 20].reshape(320, 128).astype(F32)
    return jnp.concatenate([wide[pl.ds(q, RANK, stride=5), :] for q in range(5)], axis=1).astype(BF16)

def conv_base(window, weight, latents, base):
    base[...] = latents[0].reshape(POS, CH).astype(F32)
    @pl.loop(0, 3)
    def _(dy):
        rows = pl.ds(pl.multiple_of(dy * WIDTH, WIDTH), POS)
        taps = pl.ds(pl.multiple_of(dy * 3 * CH, 3 * CH), 3 * CH)
        base[...] += mm(window[rows, :], weight[taps, :])

def finish(window, base, adapter, gain, wq, wk, wv, wo, out, wide, hidden_s, query, keys, values, mixed):
    unfold_down(adapter, 0, 180, wide)
    low = jnp.zeros((POS, 128), F32)
    for dy in range(3):
        low += mm(window[dy * WIDTH:dy * WIDTH + POS, :], wide[dy * 3 * CH:(dy + 1) * 3 * CH, :].astype(BF16))
    up = unfold_up(adapter, 180, wide)
    hidden = (base[...] + mm(low[:, :RANK].astype(BF16), up)).astype(BF16)
    hidden_s[...] = hidden
    h = hidden.astype(F32)
    centred = h - jnp.mean(h, axis=-1, keepdims=True)
    var = jnp.mean(centred * centred, axis=-1, keepdims=True)
    normed = (gain[...] * centred * lax.rsqrt(var + 1e-5)).astype(BF16)
    keys[0:POS, :] = mm(normed, wk[...]).astype(BF16)
    unfold_down(adapter, 200, 20, wide)
    query_low = mm(normed, wide[0:CH, :].astype(BF16))[:, :RANK].astype(BF16)
    query[...] = (mm(normed, wq[...]) + mm(query_low, unfold_up(adapter, 220, wide))).astype(BF16)
    unfold_down(adapter, 240, 20, wide)
    value_low = mm(normed, wide[0:CH, :].astype(BF16))[:, :RANK].astype(BF16)
    values[0:POS, :] = (mm(normed, wv[...]) + mm(value_low, unfold_up(adapter, 260, wide))).astype(BF16)
    scale = math.log2(math.e) / math.sqrt(CH // HEADS)
    ones = jnp.ones((2 * POS, 128), BF16)
    low_lanes = lax.broadcasted_iota(jnp.int32, (POS // BLOCKS, 128), 1) < 64
    @pl.loop(0, HEADS // 2)
    def _(pair):
        lanes = pl.ds(pl.multiple_of(pair * 128, 128), 128)
        k2 = keys[:, lanes]
        v2 = jnp.concatenate([values[:, lanes], ones], axis=1)
        for block in range(BLOCKS):
            rows = pl.ds(block * (POS // BLOCKS), POS // BLOCKS)
            q2 = query[rows, lanes]
            parts = []
            for side in (low_lanes, jnp.logical_not(low_lanes)):
                scores = lax.dot_general(jnp.where(side, q2, jnp.zeros_like(q2)), k2, (((1,), (1,)), ((), ())),
                                         preferred_element_type=F32)
                top = jnp.max(scores, axis=-1, keepdims=True)
                weights = jnp.exp2((scores - top) * scale).astype(BF16)
                got = mm(weights, v2)
                parts.append(got[:, :128] / got[:, 128:])
            mixed[rows, lanes] = jnp.where(low_lanes, parts[0], parts[1]).astype(BF16)
    result = hidden_s[...].astype(F32) + mm(mixed[...], wo[...])
    out[0] = result.astype(BF16).reshape(ROWS, WIDTH, CH)
BLOCKS = 2

def compute_kernel(latents, halo, stale, weight, gain, wq, wk, wv, wo, adapter, out,
                   window, base, wide, hidden_s, query, keys, values, mixed):
    core = lax.axis_index("patch")
    for row in range(ROWS):
        activate(row + 1, window, latents[0, row], None)
    activate(0, window, halo[...], core == 0)
    activate(ROWS + 1, window, halo[...], core == 1)
    keys[POS:, :] = stale[0, :, :CH]
    values[POS:, :] = stale[0, :, CH:]
    conv_base(window, weight, latents, base)
    finish(window, base, adapter, gain, wq, wk, wv, wo, out, wide, hidden_s, query, keys, values, mixed)

VM = pl.BlockSpec(memory_space=pltpu.VMEM)
def block(latents, halo, stale, weight, gain, wq, wk, wv, wo, adapter):
    return pl.pallas_call(
        compute_kernel,
        out_shape=jax.ShapeDtypeStruct(latents.shape, BF16),
        in_specs=[VM] * 10,
        out_specs=VM,
        scratch_shapes=[
            pltpu.VMEM(((ROWS + 2) * WIDTH, 3 * CH), BF16),
            pltpu.VMEM((POS, CH), F32),
            pltpu.VMEM((9 * CH, 128), F32),
            pltpu.VMEM((POS, CH), BF16),
            pltpu.VMEM((POS, CH), BF16),
            pltpu.VMEM((2 * POS, CH), BF16),
            pltpu.VMEM((2 * POS, CH), BF16),
            pltpu.VMEM((POS, CH), BF16),
        ],
        compiler_params=pltpu.CompilerParams(vmem_limit_bytes=56 << 20),
    )(latents, halo, stale, weight, gain.reshape(1, CH), wq, wk, wv, wo, adapter)

def body(latents, previous_key_values, convolution_kernel_weight, layer_norm_gain, query_matrix, key_matrix,
         value_matrix, output_matrix, adapter_table, request_adapter_choice, parent_request, adapter_bank_row):
    adapter, stale, halo = exchange(request_adapter_choice, parent_request, adapter_bank_row, adapter_table,
                                    previous_key_values, latents)
    return block(latents, halo, stale, convolution_kernel_weight, layer_norm_gain, query_matrix, key_matrix,
                 value_matrix, output_matrix, adapter)


def solution(mesh):
    placed = (P("req", "patch", None, None), P("req", "patch", None), P(), P(), P(), P(), P(), P(),
              P("req", None), P(), P(), P())
    return jax.shard_map(body, mesh=mesh, in_specs=placed, out_specs=P("req", "patch", None, None), check_vma=False)
```

```python
import math
import jax
import jax.numpy as jnp
from jax import lax
from jax.experimental import pallas as pl
from jax.experimental.pallas import tpu as pltpu
from jax.sharding import PartitionSpec as P

MESH = pl.DeviceIdType.MESH
F32, BF16 = jnp.float32, jnp.bfloat16
CHIPS = 128
WIDTH, ROWS, CH, RANK, HEADS = 128, 4, 640, 64, 10
POS = ROWS * WIDTH
TILE = 16 * 128
CONV, LATE = 100, 40
CONV_PLANE, LATE_PLANE, LATE_SLOT = 25, 10, 22


def mm(a, b):
    return jnp.dot(a, b, preferred_element_type=F32)


def activate(row, window, x, zero):
    act = jax.nn.silu(x.astype(F32)).astype(BF16).astype(F32)
    if zero is not None:
        act = jnp.where(zero, 0.0, act)
    at = lax.broadcasted_iota(jnp.int32, (WIDTH, CH), 0)
    spot = pl.ds(row * WIDTH, WIDTH)
    window[spot, 0:CH] = jnp.where(at == 0, 0.0, pltpu.roll(act, 1, 0)).astype(BF16)
    window[spot, CH:2 * CH] = act.astype(BF16)
    window[spot, 2 * CH:3 * CH] = jnp.where(at == WIDTH - 1, 0.0, pltpu.roll(act, WIDTH - 1, 0)).astype(BF16)


def unfold_down(adapter, first, tiles, wide, start):
    pairs = adapter[first:first + tiles].reshape(tiles * 16, 128).astype(F32)
    wide[pl.ds(start, tiles * 16, stride=2), :] = pairs
    wide[pl.ds(start + 1, tiles * 16, stride=2), :] = pltpu.roll(pairs, RANK, 1)


def unfold_up(adapter, first, tall, start):
    tall[start:start + 320, :] = adapter[first:first + 20].reshape(320, 128).astype(F32)
    return jnp.concatenate([tall[pl.ds(start + q, RANK, stride=5), :] for q in range(5)], axis=1).astype(BF16)


def kernel(choice_h, parent_h, bank_h, table_h, kv_h, latents_h, weight_h, gain_h, wq_h, wk_h, wv_h, wo_h, out,
           choice, parent, bank, stage, latents, weight, gain, wq, wk, wv, wo,
           source, spread, picked, late_spread, late_picked, adapter, halo,
           window, base, wide, tall, low, hidden_s, query, keys, values, mixed,
           load, spread_sem, pick_sem, late_spread_sem, late_pick_sem, link):
    me = lax.axis_index("req")
    core = lax.axis_index("patch")
    other = {"patch": 1 - core}
    y = lax.div(me, 32)
    slot = lax.rem(13 * lax.rem(me, 32) + 8 * y + 16 * core, 32)

    barrier = pltpu.get_barrier_semaphore()
    pl.semaphore_signal(barrier, inc=1, device_id=other, device_id_type=MESH)

    @pl.loop(1, CHIPS)
    def _(k):
        pl.semaphore_signal(barrier, inc=1, device_id={"req": lax.rem(me + k, CHIPS)}, device_id_type=MESH)

    def local(source_ref, target_ref, index):
        copy = pltpu.make_async_copy(source_ref, target_ref, load.at[index])
        copy.start()
        return copy

    first = pl.multiple_of(core * (CONV * TILE), CONV * TILE)
    table_conv = local(table_h.at[:, pl.ds(first, CONV * TILE)], stage.at[:, pl.ds(0, CONV * TILE)], 0)
    first = pl.multiple_of(2 * CONV * TILE + core * (LATE * TILE), LATE * TILE)
    table_late = local(table_h.at[:, pl.ds(first, LATE * TILE)], stage.at[:, pl.ds(CONV * TILE, LATE * TILE)], 1)
    ids = [local(choice_h, choice, 2), local(parent_h, parent, 3), local(bank_h, bank, 4)]
    lat_copy = local(latents_h.at[0], latents, 5)
    weight_copies = [local(weight_h.at[pl.ds(dy * 3 * CH, 3 * CH)], weight.at[pl.ds(dy * 3 * CH, 3 * CH)], 6 + dy)
                     for dy in range(3)]
    later = [local(a, b, 9 + i) for i, (a, b) in
             enumerate([(gain_h, gain), (wk_h, wk), (wq_h, wq), (wv_h, wv), (wo_h, wo)])]

    def compact(t):
        at = pl.multiple_of(t * TILE, TILE)
        source[t] = stage[:, pl.ds(at, TILE)].astype(F32).reshape(16, 128).astype(BF16)

    def wait_tiles(count, sem):
        tiles = source.at[pl.ds(0, count)]
        pltpu.make_async_copy(tiles, tiles, sem).wait()

    def to_partner(source_ref, target_ref, index):
        copy = pltpu.make_async_remote_copy(source_ref, target_ref, link.at[2 * index], link.at[2 * index + 1],
                                            device_id=other, device_id_type=MESH)
        copy.start()
        return copy

    table_conv.wait()
    pl.loop(0, CONV, unroll=4)(compact)
    pl.semaphore_wait(barrier, CHIPS)
    halo_copy = to_partner(latents_h.at[0, 3 * (1 - core)], halo, 0)

    def spread_out(per_plane, first_slot, first_tile, target, sem):
        @pl.loop(0, 4 * per_plane)
        def _(i):
            plane = lax.rem(y + lax.div(i, per_plane), 4)
            s = lax.rem(slot + i, per_plane)
            d = plane * 32 + lax.rem(5 * (s + first_slot + 64 - 8 * plane - 16 * core), 32)
            t = first_tile + plane * per_plane + s

            @pl.when(d != me)
            def _():
                pltpu.make_async_remote_copy(source.at[t], target.at[me], sem.at[0], sem.at[1],
                                             device_id={"req": d}, device_id_type=MESH).start()

    spread_out(CONV_PLANE, 0, 0, spread, spread_sem)
    table_late.wait()
    pl.loop(CONV, CONV + LATE, unroll=4)(compact)
    spread_out(LATE_PLANE, LATE_SLOT, CONV, late_spread, late_spread_sem)
    stale_keys = to_partner(kv_h.at[0, :, pl.ds(0, CH)], keys.at[pl.ds(POS, POS)], 1)
    stale_values = to_partner(kv_h.at[0, :, pl.ds(CH, CH)], values.at[pl.ds(POS, POS)], 2)
    holds = slot < CONV_PLANE
    holds_late = slot >= LATE_SLOT

    lat_copy.wait()
    for row in range(ROWS):
        activate(row + 1, window, latents[row], None)
    halo_copy.wait()
    activate(0, window, halo[...], core == 0)
    activate(ROWS + 1, window, halo[...], core == 1)
    base[...] = latents[...].reshape(POS, CH).astype(F32)

    def convolve(dy):
        weight_copies[dy].wait()
        base[...] += mm(window[dy * WIDTH:dy * WIDTH + POS, :], weight[dy * 3 * CH:(dy + 1) * 3 * CH, :])

    convolve(0)
    convolve(1)
    for copy in ids:
        copy.wait()

    def pick_out(mine, mine_tile, received, chosen, tile, in_sem, out_sem):
        received[me] = source[mine]
        wait_tiles(CHIPS - 1, in_sem.at[1])

        @pl.loop(0, CHIPS, unroll=4)
        def _(p):
            chosen[p] = received[bank[choice[parent[p]]]]

        @pl.loop(1, CHIPS)
        def _(k):
            d = lax.rem(me + k, CHIPS)
            pltpu.make_async_remote_copy(chosen.at[d], adapter.at[tile], out_sem.at[0], out_sem.at[1],
                                         device_id={"req": d}, device_id_type=MESH).start()
        adapter[tile] = chosen[me]

    @pl.when(holds)
    def _():
        at = CONV_PLANE * y + slot
        pick_out(at, at, spread, picked, CONV * core + at, spread_sem, pick_sem)

    @pl.when(holds_late)
    def _():
        at = LATE_PLANE * y + slot - LATE_SLOT
        pick_out(CONV + at, at, late_spread, late_picked, 2 * CONV + LATE * core + at, late_spread_sem, late_pick_sem)

    convolve(2)

    def wait_split(count, own, sem):
        @pl.when(own)
        def _():
            wait_tiles(count - 1, sem)

        @pl.when(jnp.logical_not(own))
        def _():
            wait_tiles(count, sem)

    wait_split(CONV, holds, pick_sem.at[1])
    half = adapter.at[pl.ds(CONV * core, CONV)]
    conv_forward = to_partner(half, half, 3)

    def low_part(part):
        if part == 0:
            unfold_down(adapter, 0, CONV, wide, 0)
            got = mm(window[0:POS, :], wide[0:3 * CH, :].astype(BF16))
            return got + mm(window[WIDTH:WIDTH + POS, 0:2 * CH], wide[3 * CH:5 * CH, :].astype(BF16))
        unfold_down(adapter, CONV, 80, wide, 5 * CH)
        got = mm(window[WIDTH:WIDTH + POS, 2 * CH:3 * CH], wide[5 * CH:6 * CH, :].astype(BF16))
        return got + mm(window[2 * WIDTH:2 * WIDTH + POS, :], wide[6 * CH:9 * CH, :].astype(BF16))

    @pl.when(core == 0)
    def _():
        low[...] = low_part(0)

    @pl.when(core == 1)
    def _():
        low[...] = low_part(1)

    conv_forward.wait()

    @pl.when(core == 0)
    def _():
        low[...] += low_part(1)

    @pl.when(core == 1)
    def _():
        low[...] += low_part(0)

    up = unfold_up(adapter, 180, tall, 0)
    hidden = (base[...] + mm(low[...][:, :RANK].astype(BF16), up)).astype(BF16)
    hidden_s[...] = hidden
    for copy in later:
        copy.wait()
    h = hidden.astype(F32)
    centred = h - jnp.mean(h, axis=-1, keepdims=True)
    var = jnp.mean(centred * centred, axis=-1, keepdims=True)
    normed = (gain[...].reshape(1, CH) * centred * lax.rsqrt(var + 1e-5)).astype(BF16)

    wait_split(LATE, holds_late, late_pick_sem.at[1])
    half = adapter.at[pl.ds(2 * CONV + LATE * core, LATE)]
    late_forward = to_partner(half, half, 4)
    stale_keys.wait()
    stale_values.wait()
    keys[0:POS, :] = mm(normed, wk[...]).astype(BF16)
    late_forward.wait()
    unfold_down(adapter, 200, 20, wide, 0)
    query_low = mm(normed, wide[0:CH, :].astype(BF16))[:, :RANK].astype(BF16)
    query[...] = (mm(normed, wq[...]) + mm(query_low, unfold_up(adapter, 220, tall, 320))).astype(BF16)
    unfold_down(adapter, 240, 20, wide, CH)
    value_low = mm(normed, wide[CH:2 * CH, :].astype(BF16))[:, :RANK].astype(BF16)
    values[0:POS, :] = (mm(normed, wv[...]) + mm(value_low, unfold_up(adapter, 260, tall, 640))).astype(BF16)

    scale = math.log2(math.e) / math.sqrt(CH // HEADS)
    block = POS // 2
    ones = jnp.ones((2 * POS, 128), BF16)
    low_lanes = lax.broadcasted_iota(jnp.int32, (block, 128), 1) < RANK

    @pl.loop(0, HEADS // 2, unroll=HEADS // 2)
    def _(pair):
        lanes = pl.ds(pl.multiple_of(pair * 128, 128), 128)
        k2 = keys[:, lanes]
        v2 = jnp.concatenate([values[:, lanes], ones], axis=1)
        for part in range(2):
            rows = pl.ds(part * block, block)
            q2 = query[rows, lanes]
            heads = []
            for side in (low_lanes, jnp.logical_not(low_lanes)):
                scores = lax.dot_general(jnp.where(side, q2, jnp.zeros_like(q2)), k2, (((1,), (1,)), ((), ())),
                                         preferred_element_type=F32)
                top = jnp.max(scores, axis=-1, keepdims=True)
                weights = jnp.exp2((scores - top) * scale).astype(BF16)
                got = mm(weights, v2)
                heads.append(got[:, :128] / got[:, 128:])
            mixed[rows, lanes] = jnp.where(low_lanes, heads[0], heads[1]).astype(BF16)

    result = hidden_s[...].astype(F32) + mm(mixed[...], wo[...])
    out[0] = result.astype(BF16).reshape(ROWS, WIDTH, CH)

    wait_split(CONV, holds, spread_sem.at[0])
    wait_split(LATE, holds_late, late_spread_sem.at[0])

    @pl.when(holds)
    def _():
        wait_tiles(CHIPS - 1, pick_sem.at[0])

    @pl.when(holds_late)
    def _():
        wait_tiles(CHIPS - 1, late_pick_sem.at[0])


def body(latents, previous_key_values, convolution_kernel_weight, layer_norm_gain, query_matrix, key_matrix,
         value_matrix, output_matrix, adapter_table, request_adapter_choice, parent_request, adapter_bank_row):
    here = pl.BlockSpec(memory_space=pltpu.HBM)
    tiles = pltpu.VMEM((CHIPS, 16, 128), BF16)
    square = pltpu.VMEM((CH, CH), BF16)
    return pl.pallas_call(
        kernel,
        out_shape=jax.ShapeDtypeStruct(latents.shape, BF16),
        in_specs=[here] * 12,
        out_specs=pl.BlockSpec(memory_space=pltpu.VMEM),
        scratch_shapes=[
            pltpu.SMEM((CHIPS,), jnp.int32), pltpu.SMEM((CHIPS,), jnp.int32), pltpu.SMEM((CHIPS,), jnp.int32),
            pltpu.VMEM((1, (CONV + LATE) * TILE), BF16),
            pltpu.VMEM((ROWS, WIDTH, CH), BF16),
            pltpu.VMEM((9 * CH, CH), BF16),
            pltpu.VMEM((CH,), F32),
            square, square, square, square,
            pltpu.VMEM((CONV + LATE, 16, 128), BF16),
            tiles, tiles, tiles, tiles,
            pltpu.VMEM((2 * (CONV + LATE), 16, 128), BF16),
            pltpu.VMEM((WIDTH, CH), BF16),
            pltpu.VMEM(((ROWS + 2) * WIDTH, 3 * CH), BF16),
            pltpu.VMEM((POS, CH), F32),
            pltpu.VMEM((9 * CH, 128), F32),
            pltpu.VMEM((960, 128), F32),
            pltpu.VMEM((POS, 128), F32),
            pltpu.VMEM((POS, CH), BF16),
            pltpu.VMEM((POS, CH), BF16),
            pltpu.VMEM((2 * POS, CH), BF16),
            pltpu.VMEM((2 * POS, CH), BF16),
            pltpu.VMEM((POS, CH), BF16),
            pltpu.SemaphoreType.DMA((14,)),
            pltpu.SemaphoreType.DMA((2,)),
            pltpu.SemaphoreType.DMA((2,)),
            pltpu.SemaphoreType.DMA((2,)),
            pltpu.SemaphoreType.DMA((2,)),
            pltpu.SemaphoreType.DMA((10,)),
        ],
        compiler_params=pltpu.CompilerParams(collective_id=0, has_side_effects=True, vmem_limit_bytes=58 << 20),
    )(request_adapter_choice, parent_request, adapter_bank_row, adapter_table, previous_key_values, latents,
      convolution_kernel_weight, layer_norm_gain, query_matrix, key_matrix, value_matrix, output_matrix)


def solution(mesh):
    placed = (P("req", "patch", None, None), P("req", "patch", None), P(), P(), P(), P(), P(), P(),
              P("req", None), P(), P(), P())
    return jax.shard_map(body, mesh=mesh, in_specs=placed, out_specs=P("req", "patch", None, None), check_vma=False)
```

```python
import math
import jax
import jax.numpy as jnp
from jax import lax
from jax.experimental import pallas as pl
from jax.experimental.pallas import tpu as pltpu
from jax.sharding import PartitionSpec as P

MESH = pl.DeviceIdType.MESH
F32, BF16 = jnp.float32, jnp.bfloat16
CHIPS = 128
WIDTH, ROWS, CH, RANK, HEADS = 128, 4, 640, 64, 10
POS = ROWS * WIDTH
TILE = 16 * 128
CONV, LATE = 100, 40
CONV_PLANE, LATE_PLANE, LATE_SLOT = 25, 10, 22
EARLY = ((0, 13), (13, 12))
PLANES = (2, 1, 3, 0)


def mm(a, b):
    return jnp.dot(a, b, preferred_element_type=F32)


def far_first(i, size):
    step = lax.div(i + 1, 2)
    return size // 2 + jnp.where(lax.rem(i, 2) == 1, -step, step)


def activate(row, window, x, zero):
    act = jax.nn.silu(x.astype(F32)).astype(BF16).astype(F32)
    if zero is not None:
        act = jnp.where(zero, 0.0, act)
    at = lax.broadcasted_iota(jnp.int32, (WIDTH, CH), 0)
    spot = pl.ds(row * WIDTH, WIDTH)
    window[spot, 0:CH] = jnp.where(at == 0, 0.0, pltpu.roll(act, 1, 0)).astype(BF16)
    window[spot, CH:2 * CH] = act.astype(BF16)
    window[spot, 2 * CH:3 * CH] = jnp.where(at == WIDTH - 1, 0.0, pltpu.roll(act, WIDTH - 1, 0)).astype(BF16)


def unfold_down(adapter, first, tiles, wide, start):
    pairs = adapter[pl.ds(first, tiles)].reshape(tiles * 16, 128).astype(F32)
    wide[pl.ds(start, tiles * 16, stride=2), :] = pairs
    wide[pl.ds(start + 1, tiles * 16, stride=2), :] = pltpu.roll(pairs, RANK, 1)


def unfold_up(adapter, first, tall, start):
    tall[start:start + 320, :] = adapter[first:first + 20].reshape(320, 128).astype(F32)
    return jnp.concatenate([tall[pl.ds(start + q, RANK, stride=5), :] for q in range(5)], axis=1).astype(BF16)


def kernel(choice_h, parent_h, bank_h, table_h, kv_h, latents_h, weight_h, gain_h, wq_h, wk_h, wv_h, wo_h, out,
           choice, parent, bank, wanted, stage, latents, weight, gain, wq, wk, wv, wo,
           source, spread, picked, late_spread, late_picked, adapter, halo,
           window, base, wide, tall, low, hidden_s, query, keys, values, mixed,
           load, spread_sem, pick_sent, pick_sem, late_spread_sem, late_pick_sem, link):
    me = lax.axis_index("req")
    core = lax.axis_index("patch")
    other = {"patch": 1 - core}
    y = lax.div(me, 32)
    column = lax.rem(me, 32)
    z, x = lax.div(column, 4), lax.rem(column, 4)

    def slot_of(plane, at):
        return lax.rem(13 * at + 8 * plane + 16 * core, 32)

    near = [lax.rem(x + 2, 4), lax.rem(x + 1, 4), lax.rem(x + 3, 4), x]

    def serve(ahead, send):
        plane = 32 * lax.rem(y + ahead, 4)

        @pl.loop(0, 7 if ahead == 0 else 8)
        def _(i):
            send(plane + 4 * lax.rem(z + far_first(i, 8), 8), near)
        if ahead == 0:
            send(plane + 4 * z, near[:3])

    slot = slot_of(y, column)
    holds = slot < CONV_PLANE
    holds_late = slot >= LATE_SLOT

    def local(source_ref, target_ref, index):
        copy = pltpu.make_async_copy(source_ref, target_ref, load.at[index])
        copy.start()
        return copy

    first = pl.multiple_of(core * (CONV * TILE), CONV * TILE)
    table_conv = local(table_h.at[:, pl.ds(first, CONV * TILE)], stage.at[:, pl.ds(0, CONV * TILE)], 0)
    first = pl.multiple_of(2 * CONV * TILE + core * (LATE * TILE), LATE * TILE)
    table_late = local(table_h.at[:, pl.ds(first, LATE * TILE)], stage.at[:, pl.ds(CONV * TILE, LATE * TILE)], 1)
    barrier = pltpu.get_barrier_semaphore()
    pl.semaphore_signal(barrier, inc=1, device_id=other, device_id_type=MESH)

    def greet(base, columns):
        for x_to in columns:
            pl.semaphore_signal(barrier, inc=1, device_id={"req": base + x_to}, device_id_type=MESH)

    for ahead in PLANES:
        serve(ahead, greet)

    ids = [local(choice_h, choice, 2), local(parent_h, parent, 3), local(bank_h, bank, 4)]
    lat_copy = local(latents_h.at[0], latents, 5)
    weight_copies = [local(weight_h.at[pl.ds(dy * 3 * CH, 3 * CH)], weight.at[pl.ds(dy * 3 * CH, 3 * CH)], 6 + dy)
                     for dy in range(3)]
    later = [local(a, b, 9 + i) for i, (a, b) in
             enumerate([(gain_h, gain), (wk_h, wk), (wq_h, wq), (wv_h, wv), (wo_h, wo)])]

    def compact(t):
        at = pl.multiple_of(t * TILE, TILE)
        source[t] = stage[:, pl.ds(at, TILE)].astype(F32).reshape(16, 128).astype(BF16)

    def wait_tiles(count, sem):
        tiles = source.at[pl.ds(0, count)]
        pltpu.make_async_copy(tiles, tiles, sem).wait()

    def to_partner(source_ref, target_ref, index):
        copy = pltpu.make_async_remote_copy(source_ref, target_ref, link.at[2 * index], link.at[2 * index + 1],
                                            device_id=other, device_id_type=MESH)
        copy.start()
        return copy


    def compact_plane(ahead, per_plane, first_tile):
        start = first_tile + lax.rem(y + ahead, 4) * per_plane
        pl.loop(0, per_plane, unroll=5)(lambda i: compact(start + i))

    def spread_plane(ahead, first_slot, count, per_plane, first_tile, target, sem):
        plane = lax.rem(y + ahead, 4)

        @pl.loop(0, count)
        def _(i):
            s = first_slot + lax.rem(slot + i, count)
            d = 32 * plane + lax.rem(5 * (s + 64 - 8 * plane - 16 * core), 32)

            @pl.when(d != me)
            def _():
                pltpu.make_async_remote_copy(source.at[first_tile + plane * per_plane + s], target.at[me], sem.at[0],
                                             sem.at[1], device_id={"req": d}, device_id_type=MESH).start()

    table_conv.wait()
    compact_plane(PLANES[0], CONV_PLANE, 0)
    pl.semaphore_wait(barrier, CHIPS)
    halo_copy = to_partner(latents_h.at[0, 3 * (1 - core)], halo, 0)
    for turn in range(4):
        spread_plane(PLANES[turn], *EARLY[0], CONV_PLANE, 0, spread, spread_sem)
        if turn < 3:
            compact_plane(PLANES[turn + 1], CONV_PLANE, 0)
    for ahead in PLANES:
        spread_plane(ahead, *EARLY[1], CONV_PLANE, 0, spread, spread_sem)
    table_late.wait()
    for ahead in PLANES:
        compact_plane(ahead, LATE_PLANE, CONV)
        spread_plane(ahead, LATE_SLOT, LATE_PLANE, LATE_PLANE, CONV - LATE_SLOT, late_spread, late_spread_sem)
    stale_keys = to_partner(kv_h.at[0, :, pl.ds(0, CH)], keys.at[pl.ds(POS, POS)], 1)
    stale_values = to_partner(kv_h.at[0, :, pl.ds(CH, CH)], values.at[pl.ds(POS, POS)], 2)

    for copy in ids:
        copy.wait()

    @pl.loop(0, CHIPS, unroll=8)
    def _(p):
        wanted[p] = bank[choice[parent[p]]]

    lat_copy.wait()
    for row in range(ROWS):
        activate(row + 1, window, latents[row], None)
    halo_copy.wait()
    activate(0, window, halo[...], core == 0)
    activate(ROWS + 1, window, halo[...], core == 1)
    base[...] = latents[...].reshape(POS, CH).astype(F32)

    def convolve(dy):
        weight_copies[dy].wait()
        base[...] += mm(window[dy * WIDTH:dy * WIDTH + POS, :], weight[dy * 3 * CH:(dy + 1) * 3 * CH, :])

    convolve(0)

    def pick_out(mine, received, chosen, tile, in_sem, sent_sem, out_sem):
        received[me] = source[mine]
        wait_tiles(CHIPS - 1, in_sem.at[1])
        adapter[tile] = received[wanted[me]]
        for ahead in PLANES:
            def send(base, columns):
                for x_to in columns:
                    chosen[base + x_to] = received[wanted[base + x_to]]
                for x_to in columns:
                    pltpu.make_async_remote_copy(chosen.at[base + x_to], adapter.at[tile], sent_sem, out_sem(ahead),
                                                 device_id={"req": base + x_to}, device_id_type=MESH).start()
            serve(ahead, send)

    @pl.when(holds)
    def _():
        at = CONV_PLANE * y + slot
        pick_out(at, spread, picked, CONV * core + at, spread_sem, pick_sent, lambda ahead: pick_sem.at[ahead])

    @pl.when(holds_late)
    def _():
        at = LATE_PLANE * y + slot - LATE_SLOT
        pick_out(CONV + at, late_spread, late_picked, 2 * CONV + LATE * core + at, late_spread_sem,
                 late_pick_sem.at[0], lambda ahead: late_pick_sem.at[1])

    convolve(1)
    convolve(2)

    def wait_split(count, own, sem):
        @pl.when(own)
        def _():
            wait_tiles(count - 1, sem)

        @pl.when(jnp.logical_not(own))
        def _():
            wait_tiles(count, sem)

    forwards = []
    starts = []
    for ahead in PLANES:
        plane = lax.rem(y + 4 - ahead, 4)
        if ahead == 0:
            wait_split(CONV_PLANE, holds, pick_sem.at[ahead])
        else:
            wait_tiles(CONV_PLANE, pick_sem.at[ahead])
        at = CONV * core + CONV_PLANE * plane
        part = adapter.at[pl.ds(at, CONV_PLANE)]
        forwards.append(to_partner(part, part, 4 + ahead))
        unfold_down(adapter, at, CONV_PLANE, wide, at * 32)
        starts.append(CONV * (1 - core) + CONV_PLANE * plane)

    def low_part(part):
        if part == 0:
            got = mm(window[0:POS, :], wide[0:3 * CH, :].astype(BF16))
            return got + mm(window[WIDTH:WIDTH + POS, 0:2 * CH], wide[3 * CH:5 * CH, :].astype(BF16))
        got = mm(window[WIDTH:WIDTH + POS, 2 * CH:3 * CH], wide[5 * CH:6 * CH, :].astype(BF16))
        return got + mm(window[2 * WIDTH:2 * WIDTH + POS, :], wide[6 * CH:9 * CH, :].astype(BF16))

    @pl.when(core == 0)
    def _():
        low[...] = low_part(0)

    @pl.when(core == 1)
    def _():
        low[...] = low_part(1)

    for forward, at in zip(forwards, starts):
        forward.wait()
        unfold_down(adapter, at, CONV_PLANE, wide, at * 32)

    @pl.when(core == 0)
    def _():
        low[...] += low_part(1)

    @pl.when(core == 1)
    def _():
        low[...] += low_part(0)

    up = unfold_up(adapter, 180, tall, 0)
    hidden = (base[...] + mm(low[...][:, :RANK].astype(BF16), up)).astype(BF16)
    hidden_s[...] = hidden
    for copy in later:
        copy.wait()
    h = hidden.astype(F32)
    centred = h - jnp.mean(h, axis=-1, keepdims=True)
    var = jnp.mean(centred * centred, axis=-1, keepdims=True)
    normed = (gain[...].reshape(1, CH) * centred * lax.rsqrt(var + 1e-5)).astype(BF16)

    keys[0:POS, :] = mm(normed, wk[...]).astype(BF16)
    query_f = mm(normed, wq[...])
    wait_split(LATE, holds_late, late_pick_sem.at[1])
    half = adapter.at[pl.ds(2 * CONV + LATE * core, LATE)]
    late_forward = to_partner(half, half, 3)
    values_f = mm(normed, wv[...])
    stale_keys.wait()
    stale_values.wait()
    late_forward.wait()
    unfold_down(adapter, 200, 20, wide, 0)
    unfold_down(adapter, 240, 20, wide, CH)
    query_low = mm(normed, wide[0:CH, :].astype(BF16))[:, :RANK].astype(BF16)
    value_low = mm(normed, wide[CH:2 * CH, :].astype(BF16))[:, :RANK].astype(BF16)
    query[...] = (query_f + mm(query_low, unfold_up(adapter, 220, tall, 320))).astype(BF16)
    values[0:POS, :] = (values_f + mm(value_low, unfold_up(adapter, 260, tall, 640))).astype(BF16)

    scale = math.log2(math.e) / math.sqrt(CH // HEADS)
    block = POS // 2
    ones = jnp.ones((2 * POS, 128), BF16)
    low_lanes = lax.broadcasted_iota(jnp.int32, (block, 128), 1) < RANK

    @pl.loop(0, HEADS // 2, unroll=HEADS // 2)
    def _(pair):
        lanes = pl.ds(pl.multiple_of(pair * 128, 128), 128)
        k2 = keys[:, lanes]
        v2 = jnp.concatenate([values[:, lanes], ones], axis=1)
        for part in range(2):
            rows = pl.ds(part * block, block)
            q2 = query[rows, lanes]
            heads = []
            for side in (low_lanes, jnp.logical_not(low_lanes)):
                scores = lax.dot_general(jnp.where(side, q2, jnp.zeros_like(q2)), k2, (((1,), (1,)), ((), ())),
                                         preferred_element_type=F32)
                top = jnp.max(scores, axis=-1, keepdims=True)
                weights = jnp.exp2((scores - top) * scale).astype(BF16)
                got = mm(weights, v2)
                heads.append(got[:, :128] / got[:, 128:])
            mixed[rows, lanes] = jnp.where(low_lanes, heads[0], heads[1]).astype(BF16)

    result = hidden_s[...].astype(F32) + mm(mixed[...], wo[...])
    out[0] = result.astype(BF16).reshape(ROWS, WIDTH, CH)

    wait_split(CONV, holds, spread_sem.at[0])
    wait_split(LATE, holds_late, late_spread_sem.at[0])

    @pl.when(holds)
    def _():
        wait_tiles(CHIPS - 1, pick_sent)

    @pl.when(holds_late)
    def _():
        wait_tiles(CHIPS - 1, late_pick_sem.at[0])


def body(latents, previous_key_values, convolution_kernel_weight, layer_norm_gain, query_matrix, key_matrix,
         value_matrix, output_matrix, adapter_table, request_adapter_choice, parent_request, adapter_bank_row):
    here = pl.BlockSpec(memory_space=pltpu.HBM)
    ids = pltpu.SMEM((CHIPS,), jnp.int32)
    tiles = pltpu.VMEM((CHIPS, 16, 128), BF16)
    square = pltpu.VMEM((CH, CH), BF16)
    return pl.pallas_call(
        kernel,
        out_shape=jax.ShapeDtypeStruct(latents.shape, BF16),
        in_specs=[here] * 12,
        out_specs=pl.BlockSpec(memory_space=pltpu.VMEM),
        scratch_shapes=[
            ids, ids, ids, ids,
            pltpu.VMEM((1, (CONV + LATE) * TILE), BF16),
            pltpu.VMEM((ROWS, WIDTH, CH), BF16),
            pltpu.VMEM((9 * CH, CH), BF16),
            pltpu.VMEM((CH,), F32),
            square, square, square, square,
            pltpu.VMEM((CONV + LATE, 16, 128), BF16),
            tiles, tiles, tiles, tiles,
            pltpu.VMEM((2 * (CONV + LATE), 16, 128), BF16),
            pltpu.VMEM((WIDTH, CH), BF16),
            pltpu.VMEM(((ROWS + 2) * WIDTH, 3 * CH), BF16),
            pltpu.VMEM((POS, CH), F32),
            pltpu.VMEM((2 * CONV * 32, 128), F32),
            pltpu.VMEM((960, 128), F32),
            pltpu.VMEM((POS, 128), F32),
            pltpu.VMEM((POS, CH), BF16),
            pltpu.VMEM((POS, CH), BF16),
            pltpu.VMEM((2 * POS, CH), BF16),
            pltpu.VMEM((2 * POS, CH), BF16),
            pltpu.VMEM((POS, CH), BF16),
            pltpu.SemaphoreType.DMA((14,)),
            pltpu.SemaphoreType.DMA((2,)),
            pltpu.SemaphoreType.DMA,
            pltpu.SemaphoreType.DMA((4,)),
            pltpu.SemaphoreType.DMA((2,)),
            pltpu.SemaphoreType.DMA((2,)),
            pltpu.SemaphoreType.DMA((16,)),
        ],
        compiler_params=pltpu.CompilerParams(collective_id=0, has_side_effects=True, vmem_limit_bytes=58 << 20),
    )(request_adapter_choice, parent_request, adapter_bank_row, adapter_table, previous_key_values, latents,
      convolution_kernel_weight, layer_norm_gain, query_matrix, key_matrix, value_matrix, output_matrix)


def solution(mesh):
    placed = (P("req", "patch", None, None), P("req", "patch", None), P(), P(), P(), P(), P(), P(),
              P("req", None), P(), P(), P())
    return jax.shard_map(body, mesh=mesh, in_specs=placed, out_specs=P("req", "patch", None, None), check_vma=False)
```

```python
import math
import jax
import jax.numpy as jnp
from jax import lax
from jax.experimental import pallas as pl
from jax.experimental.pallas import tpu as pltpu
from jax.sharding import PartitionSpec as P

MESH = pl.DeviceIdType.MESH
F32, BF16 = jnp.float32, jnp.bfloat16
CHIPS = 128
WIDTH, ROWS, CH, RANK, HEADS = 128, 4, 640, 64, 10
POS = ROWS * WIDTH
TILE = 16 * 128
CONV, LATE = 100, 40
CONV_PLANE, LATE_PLANE, LATE_SLOT = 25, 10, 22
EARLY = ((0, 8), (8, 8), (16, 9))
PLANES = (2, 1, 3, 0)


def mm(a, b):
    return jnp.dot(a, b, preferred_element_type=F32)


def far_first(i, size):
    step = lax.div(i + 1, 2)
    return size // 2 + jnp.where(lax.rem(i, 2) == 1, -step, step)


def activate(row, window, x, zero):
    act = jax.nn.silu(x.astype(F32)).astype(BF16).astype(F32)
    if zero is not None:
        act = jnp.where(zero, 0.0, act)
    at = lax.broadcasted_iota(jnp.int32, (WIDTH, CH), 0)
    spot = pl.ds(row * WIDTH, WIDTH)
    window[spot, 0:CH] = jnp.where(at == 0, 0.0, pltpu.roll(act, 1, 0)).astype(BF16)
    window[spot, CH:2 * CH] = act.astype(BF16)
    window[spot, 2 * CH:3 * CH] = jnp.where(at == WIDTH - 1, 0.0, pltpu.roll(act, WIDTH - 1, 0)).astype(BF16)


def unfold_down(adapter, first, tiles, wide, start):
    pairs = adapter[pl.ds(first, tiles)].reshape(tiles * 16, 128).astype(F32)
    wide[pl.ds(start, tiles * 16, stride=2), :] = pairs
    wide[pl.ds(start + 1, tiles * 16, stride=2), :] = pltpu.roll(pairs, RANK, 1)


def unfold_up(adapter, first, tall, start):
    tall[start:start + 320, :] = adapter[first:first + 20].reshape(320, 128).astype(F32)
    return jnp.concatenate([tall[pl.ds(start + q, RANK, stride=5), :] for q in range(5)], axis=1).astype(BF16)


def kernel(choice_h, parent_h, bank_h, table_h, kv_h, latents_h, weight_h, gain_h, wq_h, wk_h, wv_h, wo_h, out,
           choice, parent, bank, wanted, stage, latents, weight, gain, wkqv, wo,
           source, spread, picked, late_spread, late_picked, adapter, halo,
           window, base, wide, tall, low, hidden_s, query, keys, values, mixed,
           load, spread_sem, pick_sent, pick_sem, late_spread_sem, late_pick_sem, link):
    me = lax.axis_index("req")
    core = lax.axis_index("patch")
    other = {"patch": 1 - core}
    y = lax.div(me, 32)
    column = lax.rem(me, 32)
    z, x = lax.div(column, 4), lax.rem(column, 4)

    def slot_of(plane, at):
        return lax.rem(13 * at + 9 * plane + 17 * core, 32)

    near = [lax.rem(x + 2, 4), lax.rem(x + 1, 4), lax.rem(x + 3, 4), x]

    def serve(ahead, send):
        plane = 32 * lax.rem(y + ahead, 4)

        @pl.loop(0, 7 if ahead == 0 else 8)
        def _(i):
            send(plane + 4 * lax.rem(z + far_first(i, 8), 8), near)
        if ahead == 0:
            send(plane + 4 * z, near[:3])

    slot = slot_of(y, column)
    holds = slot < CONV_PLANE
    holds_late = slot >= LATE_SLOT

    def local(source_ref, target_ref, index):
        copy = pltpu.make_async_copy(source_ref, target_ref, load.at[index])
        copy.start()
        return copy

    first = pl.multiple_of(core * (CONV * TILE), CONV * TILE)
    table_conv = local(table_h.at[:, pl.ds(first, CONV * TILE)], stage.at[:, pl.ds(0, CONV * TILE)], 0)
    first = pl.multiple_of(2 * CONV * TILE + core * (LATE * TILE), LATE * TILE)
    table_late = local(table_h.at[:, pl.ds(first, LATE * TILE)], stage.at[:, pl.ds(CONV * TILE, LATE * TILE)], 1)
    barrier = pltpu.get_barrier_semaphore()
    pl.semaphore_signal(barrier, inc=1, device_id=other, device_id_type=MESH)

    def greet(base, columns):
        for x_to in columns:
            pl.semaphore_signal(barrier, inc=1, device_id={"req": base + x_to}, device_id_type=MESH)

    for ahead in PLANES:
        serve(ahead, greet)

    ids = [local(choice_h, choice, 2), local(parent_h, parent, 3), local(bank_h, bank, 4)]
    lat_copy = local(latents_h.at[0], latents, 5)
    weight_copies = [local(weight_h.at[pl.ds(dy * 3 * CH, 3 * CH)], weight.at[pl.ds(dy * 3 * CH, 3 * CH)], 6 + dy)
                     for dy in range(3)]
    later = [local(a, b, 9 + i) for i, (a, b) in
             enumerate([(gain_h, gain), (wk_h, wkqv.at[:, pl.ds(0, CH)]), (wq_h, wkqv.at[:, pl.ds(CH, CH)]),
                        (wv_h, wkqv.at[:, pl.ds(2 * CH, CH)]), (wo_h, wo)])]

    def compact(t):
        at = pl.multiple_of(t * TILE, TILE)
        source[t] = stage[:, pl.ds(at, TILE)].astype(F32).reshape(16, 128).astype(BF16)

    def wait_tiles(count, sem):
        tiles = source.at[pl.ds(0, count)]
        pltpu.make_async_copy(tiles, tiles, sem).wait()

    def to_partner(source_ref, target_ref, index):
        copy = pltpu.make_async_remote_copy(source_ref, target_ref, link.at[2 * index], link.at[2 * index + 1],
                                            device_id=other, device_id_type=MESH)
        copy.start()
        return copy


    def compact_plane(ahead, per_plane, first_tile):
        start = first_tile + lax.rem(y + ahead, 4) * per_plane
        pl.loop(0, per_plane, unroll=5)(lambda i: compact(start + i))

    def spread_plane(ahead, first_slot, count, per_plane, first_tile, target, sem):
        plane = lax.rem(y + ahead, 4)

        def send(base, columns):
            shift = 13 * (base - 32 * plane) + 9 * plane + 17 * core
            for x_to in columns:
                s = lax.rem(shift + 13 * x_to, 32)

                @pl.when(jnp.logical_and(s >= first_slot, s < first_slot + count))
                def _():
                    pltpu.make_async_remote_copy(source.at[first_tile + plane * per_plane + s], target.at[me], sem.at[0],
                                                 sem.at[1], device_id={"req": base + x_to}, device_id_type=MESH).start()
        serve(ahead, send)

    table_conv.wait()
    compact_plane(PLANES[0], CONV_PLANE, 0)
    pl.semaphore_wait(barrier, CHIPS)
    halo_copy = to_partner(latents_h.at[0, 3 * (1 - core)], halo, 0)
    for turn in range(4):
        spread_plane(PLANES[turn], *EARLY[0], CONV_PLANE, 0, spread, spread_sem)
        if turn < 3:
            compact_plane(PLANES[turn + 1], CONV_PLANE, 0)
    for group in EARLY[1:]:
        for ahead in PLANES:
            spread_plane(ahead, *group, CONV_PLANE, 0, spread, spread_sem)
    table_late.wait()
    for ahead in PLANES:
        compact_plane(ahead, LATE_PLANE, CONV)
        spread_plane(ahead, LATE_SLOT, LATE_PLANE, LATE_PLANE, CONV - LATE_SLOT, late_spread, late_spread_sem)
    stale_keys = to_partner(kv_h.at[0, :, pl.ds(0, CH)], keys.at[pl.ds(POS, POS)], 1)
    stale_values = to_partner(kv_h.at[0, :, pl.ds(CH, CH)], values.at[pl.ds(POS, POS)], 2)

    for copy in ids:
        copy.wait()

    @pl.loop(0, CHIPS, unroll=8)
    def _(p):
        wanted[p] = bank[choice[parent[p]]]

    lat_copy.wait()
    for row in range(ROWS):
        activate(row + 1, window, latents[row], None)
    halo_copy.wait()
    activate(0, window, halo[...], core == 0)
    activate(ROWS + 1, window, halo[...], core == 1)
    base[...] = latents[...].reshape(POS, CH).astype(F32)

    def convolve(dy):
        weight_copies[dy].wait()
        base[...] += mm(window[dy * WIDTH:dy * WIDTH + POS, :], weight[dy * 3 * CH:(dy + 1) * 3 * CH, :])

    def pick_out(mine, received, chosen, tile, in_sem, sent_sem, out_sem):
        received[me] = source[mine]
        wait_tiles(CHIPS - 1, in_sem.at[1])
        adapter[tile] = received[wanted[me]]
        for ahead in PLANES:
            def send(base, columns):
                for x_to in columns:
                    chosen[base + x_to] = received[wanted[base + x_to]]
                for x_to in columns:
                    pltpu.make_async_remote_copy(chosen.at[base + x_to], adapter.at[tile], sent_sem, out_sem(ahead),
                                                 device_id={"req": base + x_to}, device_id_type=MESH).start()
            serve(ahead, send)

    def pick_conv():
        at = CONV_PLANE * y + slot
        pick_out(at, spread, picked, CONV * core + at, spread_sem, pick_sent, lambda ahead: pick_sem.at[ahead])

    pl.when(slot < EARLY[1][0])(pick_conv)
    convolve(0)
    pl.when(jnp.logical_and(holds, slot >= EARLY[1][0]))(pick_conv)

    @pl.when(holds_late)
    def _():
        at = LATE_PLANE * y + slot - LATE_SLOT
        pick_out(CONV + at, late_spread, late_picked, 2 * CONV + LATE * core + at, late_spread_sem,
                 late_pick_sem.at[0], lambda ahead: late_pick_sem.at[1])

    convolve(1)
    convolve(2)

    def wait_split(count, own, sem):
        @pl.when(own)
        def _():
            wait_tiles(count - 1, sem)

        @pl.when(jnp.logical_not(own))
        def _():
            wait_tiles(count, sem)

    forwards = []
    starts = []
    for ahead in PLANES:
        plane = lax.rem(y + 4 - ahead, 4)
        if ahead == 0:
            wait_split(CONV_PLANE, holds, pick_sem.at[ahead])
        else:
            wait_tiles(CONV_PLANE, pick_sem.at[ahead])
        at = CONV * core + CONV_PLANE * plane
        part = adapter.at[pl.ds(at, CONV_PLANE)]
        forwards.append(to_partner(part, part, 4 + ahead))
        unfold_down(adapter, at, CONV_PLANE, wide, at * 32)
        starts.append(CONV * (1 - core) + CONV_PLANE * plane)

    def low_part(part):
        if part == 0:
            got = mm(window[0:POS, :], wide[0:3 * CH, :].astype(BF16))
            return got + mm(window[WIDTH:WIDTH + POS, 0:2 * CH], wide[3 * CH:5 * CH, :].astype(BF16))
        got = mm(window[WIDTH:WIDTH + POS, 2 * CH:3 * CH], wide[5 * CH:6 * CH, :].astype(BF16))
        return got + mm(window[2 * WIDTH:2 * WIDTH + POS, :], wide[6 * CH:9 * CH, :].astype(BF16))

    @pl.when(core == 0)
    def _():
        low[...] = low_part(0)

    @pl.when(core == 1)
    def _():
        low[...] = low_part(1)

    for forward, at in zip(forwards, starts):
        forward.wait()
        unfold_down(adapter, at, CONV_PLANE, wide, at * 32)

    @pl.when(core == 0)
    def _():
        low[...] += low_part(1)

    @pl.when(core == 1)
    def _():
        low[...] += low_part(0)

    up = unfold_up(adapter, 180, tall, 0)
    hidden = (base[...] + mm(low[...][:, :RANK].astype(BF16), up)).astype(BF16)
    hidden_s[...] = hidden
    for copy in later:
        copy.wait()
    h = hidden.astype(F32)
    centred = h - jnp.mean(h, axis=-1, keepdims=True)
    var = jnp.mean(centred * centred, axis=-1, keepdims=True)
    normed = (gain[...].reshape(1, CH) * centred * lax.rsqrt(var + 1e-5)).astype(BF16)

    projected = mm(normed, wkqv[...])
    keys[0:POS, :] = projected[:, :CH].astype(BF16)
    wait_split(LATE, holds_late, late_pick_sem.at[1])
    half = adapter.at[pl.ds(2 * CONV + LATE * core, LATE)]
    late_forward = to_partner(half, half, 3)
    stale_keys.wait()
    stale_values.wait()
    late_forward.wait()
    unfold_down(adapter, 200, 20, wide, 0)
    unfold_down(adapter, 240, 20, wide, CH)
    downs = [wide[0:CH, :].astype(BF16), wide[CH:2 * CH, :].astype(BF16)]
    lows = mm(normed, jnp.concatenate(downs, axis=1)).astype(BF16)
    query[...] = (projected[:, CH:2 * CH] + mm(lows[:, :RANK], unfold_up(adapter, 220, tall, 320))).astype(BF16)
    values[0:POS, :] = (projected[:, 2 * CH:] + mm(lows[:, 128:128 + RANK], unfold_up(adapter, 260, tall, 640))).astype(BF16)

    scale = math.log2(math.e) / math.sqrt(CH // HEADS)
    block = POS // 2
    ones = jnp.ones((2 * POS, 128), BF16)
    low_lanes = lax.broadcasted_iota(jnp.int32, (block, 128), 1) < RANK

    @pl.loop(0, HEADS // 2, unroll=HEADS // 2)
    def _(pair):
        lanes = pl.ds(pl.multiple_of(pair * 128, 128), 128)
        k2 = keys[:, lanes]
        v2 = jnp.concatenate([values[:, lanes], ones], axis=1)
        for part in range(2):
            rows = pl.ds(part * block, block)
            q2 = query[rows, lanes]
            heads = []
            for side in (low_lanes, jnp.logical_not(low_lanes)):
                scores = lax.dot_general(jnp.where(side, q2, jnp.zeros_like(q2)), k2, (((1,), (1,)), ((), ())),
                                         preferred_element_type=F32)
                top = jnp.max(scores, axis=-1, keepdims=True)
                weights = jnp.exp2((scores - top) * scale).astype(BF16)
                heads.append(mm(weights, v2))
            total = jnp.where(low_lanes, heads[0][:, 128:], heads[1][:, 128:])
            mixed[rows, lanes] = (jnp.where(low_lanes, heads[0][:, :128], heads[1][:, :128]) / total).astype(BF16)

    leaving = []
    for part in range(2):
        rows, image = pl.ds(part * block, block), pl.ds(part * (ROWS // 2), ROWS // 2)
        result = hidden_s[rows, :].astype(F32) + mm(mixed[rows, :], wo[...])
        latents[image] = result.astype(BF16).reshape(ROWS // 2, WIDTH, CH)
        leaving.append(local(latents.at[image], out.at[0, image], 14 + part))

    for copy in leaving:
        copy.wait()
    wait_split(CONV, holds, spread_sem.at[0])
    wait_split(LATE, holds_late, late_spread_sem.at[0])

    @pl.when(holds)
    def _():
        wait_tiles(CHIPS - 1, pick_sent)

    @pl.when(holds_late)
    def _():
        wait_tiles(CHIPS - 1, late_pick_sem.at[0])


def body(latents, previous_key_values, convolution_kernel_weight, layer_norm_gain, query_matrix, key_matrix,
         value_matrix, output_matrix, adapter_table, request_adapter_choice, parent_request, adapter_bank_row):
    here = pl.BlockSpec(memory_space=pltpu.HBM)
    ids = pltpu.SMEM((CHIPS,), jnp.int32)
    tiles = pltpu.VMEM((CHIPS, 16, 128), BF16)
    return pl.pallas_call(
        kernel,
        out_shape=jax.ShapeDtypeStruct(latents.shape, BF16),
        in_specs=[here] * 12,
        out_specs=here,
        scratch_shapes=[
            ids, ids, ids, ids,
            pltpu.VMEM((1, (CONV + LATE) * TILE), BF16),
            pltpu.VMEM((ROWS, WIDTH, CH), BF16),
            pltpu.VMEM((9 * CH, CH), BF16),
            pltpu.VMEM((CH,), F32),
            pltpu.VMEM((CH, 3 * CH), BF16),
            pltpu.VMEM((CH, CH), BF16),
            pltpu.VMEM((CONV + LATE, 16, 128), BF16),
            tiles, tiles, tiles, tiles,
            pltpu.VMEM((2 * (CONV + LATE), 16, 128), BF16),
            pltpu.VMEM((WIDTH, CH), BF16),
            pltpu.VMEM(((ROWS + 2) * WIDTH, 3 * CH), BF16),
            pltpu.VMEM((POS, CH), F32),
            pltpu.VMEM((2 * CONV * 32, 128), F32),
            pltpu.VMEM((960, 128), F32),
            pltpu.VMEM((POS, 128), F32),
            pltpu.VMEM((POS, CH), BF16),
            pltpu.VMEM((POS, CH), BF16),
            pltpu.VMEM((2 * POS, CH), BF16),
            pltpu.VMEM((2 * POS, CH), BF16),
            pltpu.VMEM((POS, CH), BF16),
            pltpu.SemaphoreType.DMA((16,)),
            pltpu.SemaphoreType.DMA((2,)),
            pltpu.SemaphoreType.DMA,
            pltpu.SemaphoreType.DMA((4,)),
            pltpu.SemaphoreType.DMA((2,)),
            pltpu.SemaphoreType.DMA((2,)),
            pltpu.SemaphoreType.DMA((16,)),
        ],
        compiler_params=pltpu.CompilerParams(collective_id=0, has_side_effects=True, vmem_limit_bytes=58 << 20),
    )(request_adapter_choice, parent_request, adapter_bank_row, adapter_table, previous_key_values, latents,
      convolution_kernel_weight, layer_norm_gain, query_matrix, key_matrix, value_matrix, output_matrix)


def solution(mesh):
    placed = (P("req", "patch", None, None), P("req", "patch", None), P(), P(), P(), P(), P(), P(),
              P("req", None), P(), P(), P())
    return jax.shard_map(body, mesh=mesh, in_specs=placed, out_specs=P("req", "patch", None, None), check_vma=False)
```

```python
import math
import jax
import jax.numpy as jnp
from jax import lax
from jax.experimental import pallas as pl
from jax.experimental.pallas import tpu as pltpu
from jax.sharding import PartitionSpec as P

MESH = pl.DeviceIdType.MESH
F32, BF16 = jnp.float32, jnp.bfloat16
CHIPS = 128
WIDTH, ROWS, CH, RANK, HEADS = 128, 4, 640, 64, 10
POS = ROWS * WIDTH
TILE = 16 * 128
CONV, LATE = 100, 40
CONV_PLANE, LATE_PLANE, LATE_SLOT = 25, 10, 22
EARLY = ((0, 8), (8, 8), (16, 9))
PLANES = (2, 1, 3, 0)


def mm(a, b):
    return jnp.dot(a, b, preferred_element_type=F32)


def far_first(i, size):
    step = lax.div(i + 1, 2)
    return size // 2 + jnp.where(lax.rem(i, 2) == 1, -step, step)


def activate(row, window, x, zero):
    act = jax.nn.silu(x.astype(F32)).astype(BF16).astype(F32)
    if zero is not None:
        act = jnp.where(zero, 0.0, act)
    at = lax.broadcasted_iota(jnp.int32, (WIDTH, CH), 0)
    spot = pl.ds(row * WIDTH, WIDTH)
    window[spot, 0:CH] = jnp.where(at == 0, 0.0, pltpu.roll(act, 1, 0)).astype(BF16)
    window[spot, CH:2 * CH] = act.astype(BF16)
    window[spot, 2 * CH:3 * CH] = jnp.where(at == WIDTH - 1, 0.0, pltpu.roll(act, WIDTH - 1, 0)).astype(BF16)


def unfold_down(adapter, first, tiles, wide, start):
    pairs = adapter[pl.ds(first, tiles)].reshape(tiles * 16, 128).astype(F32)
    wide[pl.ds(start, tiles * 16, stride=2), :] = pairs
    wide[pl.ds(start + 1, tiles * 16, stride=2), :] = pltpu.roll(pairs, RANK, 1)


def unfold_up(adapter, first, tall, start):
    tall[start:start + 320, :] = adapter[first:first + 20].reshape(320, 128).astype(F32)
    return jnp.concatenate([tall[pl.ds(start + q, RANK, stride=5), :] for q in range(5)], axis=1).astype(BF16)


def kernel(choice_h, parent_h, bank_h, table_h, kv_h, latents_h, weight_h, gain_h, wq_h, wk_h, wv_h, wo_h, out,
           choice, parent, bank, wanted, stage, latents, weight, gain, wkqv, wo,
           source, spread, picked, late_spread, late_picked, adapter, halo,
           window, base, wide, tall, low, hidden_s, query, keys, values, mixed,
           load, spread_sem, pick_sent, pick_sem, late_spread_sem, late_pick_sem, link):
    me = lax.axis_index("req")
    core = lax.axis_index("patch")
    other = {"patch": 1 - core}
    y = lax.div(me, 32)
    column = lax.rem(me, 32)
    z, x = lax.div(column, 4), lax.rem(column, 4)

    def slot_of(plane, at):
        return lax.rem(13 * at + 9 * plane + 17 * core, 32)

    near = [lax.rem(x + 2, 4), lax.rem(x + 1, 4), lax.rem(x + 3, 4), x]

    def serve(ahead, send):
        plane = 32 * lax.rem(y + ahead, 4)

        @pl.loop(0, 7 if ahead == 0 else 8)
        def _(i):
            send(plane + 4 * lax.rem(z + far_first(i, 8), 8), near)
        if ahead == 0:
            send(plane + 4 * z, near[:3])

    slot = slot_of(y, column)
    holds = slot < CONV_PLANE
    holds_late = slot >= LATE_SLOT

    def local(source_ref, target_ref, index):
        copy = pltpu.make_async_copy(source_ref, target_ref, load.at[index])
        copy.start()
        return copy

    first = pl.multiple_of(core * (CONV * TILE), CONV * TILE)
    table_conv = local(table_h.at[:, pl.ds(first, CONV * TILE)], stage.at[:, pl.ds(0, CONV * TILE)], 0)
    first = pl.multiple_of(2 * CONV * TILE + core * (LATE * TILE), LATE * TILE)
    table_late = local(table_h.at[:, pl.ds(first, LATE * TILE)], stage.at[:, pl.ds(CONV * TILE, LATE * TILE)], 1)
    barrier = pltpu.get_barrier_semaphore()
    pl.semaphore_signal(barrier, inc=1, device_id=other, device_id_type=MESH)

    def greet(base, columns):
        for x_to in columns:
            pl.semaphore_signal(barrier, inc=1, device_id={"req": base + x_to}, device_id_type=MESH)

    for ahead in PLANES:
        serve(ahead, greet)

    ids = [local(choice_h, choice, 2), local(parent_h, parent, 3), local(bank_h, bank, 4)]
    lat_copy = local(latents_h.at[0], latents, 5)
    weight_copies = [local(weight_h.at[pl.ds(dy * 3 * CH, 3 * CH)], weight.at[pl.ds(dy * 3 * CH, 3 * CH)], 6 + dy)
                     for dy in range(3)]
    later = [local(a, b, 9 + i) for i, (a, b) in
             enumerate([(gain_h, gain), (wk_h, wkqv.at[:, pl.ds(0, CH)]), (wq_h, wkqv.at[:, pl.ds(CH, CH)]),
                        (wv_h, wkqv.at[:, pl.ds(2 * CH, CH)]), (wo_h, wo)])]

    def compact(t):
        at = pl.multiple_of(t * TILE, TILE)
        source[t] = stage[:, pl.ds(at, TILE)].astype(F32).reshape(16, 128).astype(BF16)

    def wait_tiles(count, sem):
        tiles = source.at[pl.ds(0, count)]
        pltpu.make_async_copy(tiles, tiles, sem).wait()

    def to_partner(source_ref, target_ref, index):
        copy = pltpu.make_async_remote_copy(source_ref, target_ref, link.at[2 * index], link.at[2 * index + 1],
                                            device_id=other, device_id_type=MESH)
        copy.start()
        return copy


    def compact_plane(ahead, per_plane, first_tile):
        start = first_tile + lax.rem(y + ahead, 4) * per_plane
        pl.loop(0, per_plane, unroll=5)(lambda i: compact(start + i))

    def spread_plane(ahead, first_slot, count, per_plane, first_tile, target, sem):
        plane = lax.rem(y + ahead, 4)

        def send(base, columns):
            shift = 13 * (base - 32 * plane) + 9 * plane + 17 * core
            for x_to in columns:
                s = lax.rem(shift + 13 * x_to, 32)

                @pl.when(jnp.logical_and(s >= first_slot, s < first_slot + count))
                def _():
                    pltpu.make_async_remote_copy(source.at[first_tile + plane * per_plane + s], target.at[me], sem.at[0],
                                                 sem.at[1], device_id={"req": base + x_to}, device_id_type=MESH).start()
        serve(ahead, send)

    table_conv.wait()
    compact_plane(PLANES[0], CONV_PLANE, 0)
    pl.semaphore_wait(barrier, CHIPS)
    halo_copy = to_partner(latents_h.at[0, 3 * (1 - core)], halo, 0)
    for turn in range(4):
        spread_plane(PLANES[turn], *EARLY[0], CONV_PLANE, 0, spread, spread_sem)
        if turn < 3:
            compact_plane(PLANES[turn + 1], CONV_PLANE, 0)
    for group in EARLY[1:]:
        for ahead in PLANES:
            spread_plane(ahead, *group, CONV_PLANE, 0, spread, spread_sem)
    table_late.wait()
    for ahead in PLANES:
        compact_plane(ahead, LATE_PLANE, CONV)
        spread_plane(ahead, LATE_SLOT, LATE_PLANE, LATE_PLANE, CONV - LATE_SLOT, late_spread, late_spread_sem)
    stale_keys = to_partner(kv_h.at[0, :, pl.ds(0, CH)], keys.at[pl.ds(POS, POS)], 1)
    stale_values = to_partner(kv_h.at[0, :, pl.ds(CH, CH)], values.at[pl.ds(POS, POS)], 2)

    for copy in ids:
        copy.wait()

    @pl.loop(0, CHIPS, unroll=8)
    def _(p):
        wanted[p] = bank[choice[parent[p]]]

    lat_copy.wait()
    for row in range(ROWS):
        activate(row + 1, window, latents[row], None)
    halo_copy.wait()
    activate(0, window, halo[...], core == 0)
    activate(ROWS + 1, window, halo[...], core == 1)
    base[...] = latents[...].reshape(POS, CH).astype(F32)

    def convolve(dy):
        weight_copies[dy].wait()
        base[...] += mm(window[dy * WIDTH:dy * WIDTH + POS, :], weight[dy * 3 * CH:(dy + 1) * 3 * CH, :])

    def pick_out(mine, received, chosen, tile, in_sem, sent_sem, out_sem):
        received[me] = source[mine]
        wait_tiles(CHIPS - 1, in_sem.at[1])
        adapter[tile] = received[wanted[me]]
        for ahead in PLANES:
            def send(base, columns):
                for x_to in columns:
                    chosen[base + x_to] = received[wanted[base + x_to]]
                for x_to in columns:
                    pltpu.make_async_remote_copy(chosen.at[base + x_to], adapter.at[tile], sent_sem, out_sem(ahead),
                                                 device_id={"req": base + x_to}, device_id_type=MESH).start()
            serve(ahead, send)

    def pick_conv():
        at = CONV_PLANE * y + slot
        pick_out(at, spread, picked, CONV * core + at, spread_sem, pick_sent, lambda ahead: pick_sem.at[ahead])

    pl.when(slot < EARLY[1][0])(pick_conv)
    convolve(0)
    pl.when(jnp.logical_and(holds, slot >= EARLY[1][0]))(pick_conv)

    @pl.when(holds_late)
    def _():
        at = LATE_PLANE * y + slot - LATE_SLOT
        pick_out(CONV + at, late_spread, late_picked, 2 * CONV + LATE * core + at, late_spread_sem,
                 late_pick_sem.at[0], lambda ahead: late_pick_sem.at[1])

    convolve(1)
    convolve(2)

    def wait_split(count, own, sem):
        @pl.when(own)
        def _():
            wait_tiles(count - 1, sem)

        @pl.when(jnp.logical_not(own))
        def _():
            wait_tiles(count, sem)

    forwards = []
    starts = []
    for ahead in PLANES:
        plane = lax.rem(y + 4 - ahead, 4)
        if ahead == 0:
            wait_split(CONV_PLANE, holds, pick_sem.at[ahead])
        else:
            wait_tiles(CONV_PLANE, pick_sem.at[ahead])
        at = CONV * core + CONV_PLANE * plane
        part = adapter.at[pl.ds(at, CONV_PLANE)]
        forwards.append(to_partner(part, part, 4 + ahead))
        unfold_down(adapter, at, CONV_PLANE, wide, at * 32)
        starts.append(CONV * (1 - core) + CONV_PLANE * plane)

    def low_part(part):
        if part == 0:
            got = mm(window[0:POS, :], wide[0:3 * CH, :].astype(BF16))
            return got + mm(window[WIDTH:WIDTH + POS, 0:2 * CH], wide[3 * CH:5 * CH, :].astype(BF16))
        got = mm(window[WIDTH:WIDTH + POS, 2 * CH:3 * CH], wide[5 * CH:6 * CH, :].astype(BF16))
        return got + mm(window[2 * WIDTH:2 * WIDTH + POS, :], wide[6 * CH:9 * CH, :].astype(BF16))

    @pl.when(core == 0)
    def _():
        low[...] = low_part(0)

    @pl.when(core == 1)
    def _():
        low[...] = low_part(1)

    for forward, at in zip(forwards, starts):
        forward.wait()
        unfold_down(adapter, at, CONV_PLANE, wide, at * 32)

    @pl.when(core == 0)
    def _():
        low[...] += low_part(1)

    @pl.when(core == 1)
    def _():
        low[...] += low_part(0)

    up = unfold_up(adapter, 180, tall, 0)
    hidden = (base[...] + mm(low[...][:, :RANK].astype(BF16), up)).astype(BF16)
    hidden_s[...] = hidden
    for copy in later:
        copy.wait()
    h = hidden.astype(F32)
    centred = h - jnp.mean(h, axis=-1, keepdims=True)
    var = jnp.mean(centred * centred, axis=-1, keepdims=True)
    normed = (gain[...].reshape(1, CH) * centred * lax.rsqrt(var + 1e-5)).astype(BF16)

    projected = mm(normed, wkqv[...])
    keys[0:POS, :] = projected[:, :CH].astype(BF16)
    wait_split(LATE, holds_late, late_pick_sem.at[1])
    half = adapter.at[pl.ds(2 * CONV + LATE * core, LATE)]
    late_forward = to_partner(half, half, 3)
    stale_keys.wait()
    stale_values.wait()
    late_forward.wait()
    unfold_down(adapter, 200, 20, wide, 0)
    unfold_down(adapter, 240, 20, wide, CH)
    downs = [wide[0:CH, :].astype(BF16), wide[CH:2 * CH, :].astype(BF16)]
    lows = mm(normed, jnp.concatenate(downs, axis=1)).astype(BF16)
    query[...] = (projected[:, CH:2 * CH] + mm(lows[:, :RANK], unfold_up(adapter, 220, tall, 320))).astype(BF16)
    values[0:POS, :] = (projected[:, 2 * CH:] + mm(lows[:, 128:128 + RANK], unfold_up(adapter, 260, tall, 640))).astype(BF16)

    scale = math.log2(math.e) / math.sqrt(CH // HEADS)
    block = POS // 2
    ones = jnp.ones((2 * POS, 128), BF16)
    low_lanes = lax.broadcasted_iota(jnp.int32, (block, 128), 1) < RANK

    @pl.loop(0, HEADS // 2, unroll=HEADS // 2)
    def _(pair):
        lanes = pl.ds(pl.multiple_of(pair * 128, 128), 128)
        k2 = keys[:, lanes]
        v2 = jnp.concatenate([values[:, lanes], ones], axis=1)
        for part in range(2):
            rows = pl.ds(part * block, block)
            q2 = query[rows, lanes]
            heads = []
            for side in (low_lanes, jnp.logical_not(low_lanes)):
                scores = lax.dot_general(jnp.where(side, q2, jnp.zeros_like(q2)), k2, (((1,), (1,)), ((), ())),
                                         preferred_element_type=F32)
                top = jnp.max(scores, axis=-1, keepdims=True)
                weights = jnp.exp2((scores - top) * scale).astype(BF16)
                heads.append(mm(weights, v2))
            total = jnp.where(low_lanes, heads[0][:, 128:], heads[1][:, 128:])
            mixed[rows, lanes] = (jnp.where(low_lanes, heads[0][:, :128], heads[1][:, :128]) / total).astype(BF16)

    leaving = []
    for part in range(2):
        rows, image = pl.ds(part * block, block), pl.ds(part * (ROWS // 2), ROWS // 2)
        result = hidden_s[rows, :].astype(F32) + mm(mixed[rows, :], wo[...])
        latents[image] = result.astype(BF16).reshape(ROWS // 2, WIDTH, CH)
        leaving.append(local(latents.at[image], out.at[0, image], 14 + part))

    for copy in leaving:
        copy.wait()
    wait_split(CONV, holds, spread_sem.at[0])
    wait_split(LATE, holds_late, late_spread_sem.at[0])

    @pl.when(holds)
    def _():
        wait_tiles(CHIPS - 1, pick_sent)

    @pl.when(holds_late)
    def _():
        wait_tiles(CHIPS - 1, late_pick_sem.at[0])


def body(latents, previous_key_values, convolution_kernel_weight, layer_norm_gain, query_matrix, key_matrix,
         value_matrix, output_matrix, adapter_table, request_adapter_choice, parent_request, adapter_bank_row):
    here = pl.BlockSpec(memory_space=pltpu.HBM)
    ids = pltpu.SMEM((CHIPS,), jnp.int32)
    tiles = pltpu.VMEM((CHIPS, 16, 128), BF16)
    return pl.pallas_call(
        kernel,
        out_shape=jax.ShapeDtypeStruct(latents.shape, BF16),
        in_specs=[here] * 12,
        out_specs=pl.BlockSpec(memory_space=pl.ANY),
        scratch_shapes=[
            ids, ids, ids, ids,
            pltpu.VMEM((1, (CONV + LATE) * TILE), BF16),
            pltpu.VMEM((ROWS, WIDTH, CH), BF16),
            pltpu.VMEM((9 * CH, CH), BF16),
            pltpu.VMEM((CH,), F32),
            pltpu.VMEM((CH, 3 * CH), BF16),
            pltpu.VMEM((CH, CH), BF16),
            pltpu.VMEM((CONV + LATE, 16, 128), BF16),
            tiles, tiles, tiles, tiles,
            pltpu.VMEM((2 * (CONV + LATE), 16, 128), BF16),
            pltpu.VMEM((WIDTH, CH), BF16),
            pltpu.VMEM(((ROWS + 2) * WIDTH, 3 * CH), BF16),
            pltpu.VMEM((POS, CH), F32),
            pltpu.VMEM((2 * CONV * 32, 128), F32),
            pltpu.VMEM((960, 128), F32),
            pltpu.VMEM((POS, 128), F32),
            pltpu.VMEM((POS, CH), BF16),
            pltpu.VMEM((POS, CH), BF16),
            pltpu.VMEM((2 * POS, CH), BF16),
            pltpu.VMEM((2 * POS, CH), BF16),
            pltpu.VMEM((POS, CH), BF16),
            pltpu.SemaphoreType.DMA((16,)),
            pltpu.SemaphoreType.DMA((2,)),
            pltpu.SemaphoreType.DMA,
            pltpu.SemaphoreType.DMA((4,)),
            pltpu.SemaphoreType.DMA((2,)),
            pltpu.SemaphoreType.DMA((2,)),
            pltpu.SemaphoreType.DMA((16,)),
        ],
        compiler_params=pltpu.CompilerParams(collective_id=0, has_side_effects=True, vmem_limit_bytes=44 << 20),
    )(*[pltpu.with_memory_space_constraint(a, pltpu.HBM) for a in (
        request_adapter_choice, parent_request, adapter_bank_row, adapter_table, previous_key_values, latents,
        convolution_kernel_weight, layer_norm_gain, query_matrix, key_matrix, value_matrix, output_matrix)])


def solution(mesh):
    placed = (P("req", "patch", None, None), P("req", "patch", None), P(), P(), P(), P(), P(), P(),
              P("req", None), P(), P(), P())
    return jax.shard_map(body, mesh=mesh, in_specs=placed, out_specs=P("req", "patch", None, None), check_vma=False)
```

```python
import math
import jax
import jax.numpy as jnp
from jax import lax
from jax.experimental import pallas as pl
from jax.experimental.pallas import tpu as pltpu
from jax.sharding import PartitionSpec as P

MESH = pl.DeviceIdType.MESH
F32, BF16 = jnp.float32, jnp.bfloat16
CHIPS = 128
WIDTH, ROWS, CH, RANK, HEADS = 128, 4, 640, 64, 10
POS = ROWS * WIDTH
TILE = 16 * 128
CONV, LATE = 100, 40
CONV_PLANE, LATE_PLANE, LATE_SLOT = 25, 10, 22
EARLY = ((0, 8), (8, 8), (16, 9))
PLANES = (2, 1, 3, 0)


def mm(a, b):
    return jnp.dot(a, b, preferred_element_type=F32)


def far_first(i, size):
    step = lax.div(i + 1, 2)
    return size // 2 + jnp.where(lax.rem(i, 2) == 1, -step, step)


def activate(row, window, x, zero):
    act = jax.nn.silu(x.astype(F32)).astype(BF16).astype(F32)
    if zero is not None:
        act = jnp.where(zero, 0.0, act)
    at = lax.broadcasted_iota(jnp.int32, (WIDTH, CH), 0)
    spot = pl.ds(row * WIDTH, WIDTH)
    window[spot, 0:CH] = jnp.where(at == 0, 0.0, pltpu.roll(act, 1, 0)).astype(BF16)
    window[spot, CH:2 * CH] = act.astype(BF16)
    window[spot, 2 * CH:3 * CH] = jnp.where(at == WIDTH - 1, 0.0, pltpu.roll(act, WIDTH - 1, 0)).astype(BF16)


def unfold_down(adapter, first, tiles, wide, start):
    pairs = adapter[pl.ds(first, tiles)].reshape(tiles * 16, 128).astype(F32)
    wide[pl.ds(start, tiles * 16, stride=2), :] = pairs
    wide[pl.ds(start + 1, tiles * 16, stride=2), :] = pltpu.roll(pairs, RANK, 1)


def unfold_up(adapter, first, tall, start):
    tall[start:start + 320, :] = adapter[first:first + 20].reshape(320, 128).astype(F32)
    return jnp.concatenate([tall[pl.ds(start + q, RANK, stride=5), :] for q in range(5)], axis=1).astype(BF16)


def kernel(choice_h, parent_h, bank_h, table_h, kv_h, latents_h, weight_h, gain_h, wq_h, wk_h, wv_h, wo_h, out,
           choice, parent, bank, wanted, stage, latents, weight, gain, wkqv, wo,
           source, spread, picked, late_spread, late_picked, adapter, halo,
           window, base, wide, tall, low, hidden_s, query, keys, values, mixed,
           load, spread_sem, pick_sent, pick_sem, late_spread_sem, late_pick_sem, link):
    me = lax.axis_index("req")
    core = lax.axis_index("patch")
    other = {"patch": 1 - core}
    y = lax.div(me, 32)
    column = lax.rem(me, 32)
    z, x = lax.div(column, 4), lax.rem(column, 4)

    def slot_of(plane, at):
        return lax.rem(13 * at + 9 * plane + 17 * core, 32)

    near = [lax.rem(x + 2, 4), lax.rem(x + 1, 4), lax.rem(x + 3, 4), x]

    def serve(ahead, send):
        plane = 32 * lax.rem(y + ahead, 4)

        @pl.loop(0, 7 if ahead == 0 else 8)
        def _(i):
            send(plane + 4 * lax.rem(z + far_first(i, 8), 8), near)
        if ahead == 0:
            send(plane + 4 * z, near[:3])

    slot = slot_of(y, column)
    holds = slot < CONV_PLANE
    holds_late = slot >= LATE_SLOT

    def local(source_ref, target_ref, index):
        copy = pltpu.make_async_copy(source_ref, target_ref, load.at[index])
        copy.start()
        return copy

    first = pl.multiple_of(core * (CONV * TILE), CONV * TILE)
    table_conv = local(table_h.at[:, pl.ds(first, CONV * TILE)], stage.at[:, pl.ds(0, CONV * TILE)], 0)
    first = pl.multiple_of(2 * CONV * TILE + core * (LATE * TILE), LATE * TILE)
    table_late = local(table_h.at[:, pl.ds(first, LATE * TILE)], stage.at[:, pl.ds(CONV * TILE, LATE * TILE)], 1)
    barrier = pltpu.get_barrier_semaphore()
    pl.semaphore_signal(barrier, inc=1, device_id=other, device_id_type=MESH)

    def greet(base, columns):
        for x_to in columns:
            pl.semaphore_signal(barrier, inc=1, device_id={"req": base + x_to}, device_id_type=MESH)

    for ahead in PLANES:
        serve(ahead, greet)

    ids = [local(choice_h, choice, 2), local(parent_h, parent, 3), local(bank_h, bank, 4)]
    lat_copy = local(latents_h.at[0], latents, 5)
    weight_copies = [local(weight_h.at[pl.ds(dy * 3 * CH, 3 * CH)], weight.at[pl.ds(dy * 3 * CH, 3 * CH)], 6 + dy)
                     for dy in range(3)]
    later = [local(a, b, 9 + i) for i, (a, b) in
             enumerate([(gain_h, gain), (wk_h, wkqv.at[:, pl.ds(0, CH)]), (wq_h, wkqv.at[:, pl.ds(CH, CH)]),
                        (wv_h, wkqv.at[:, pl.ds(2 * CH, CH)]), (wo_h, wo)])]

    def compact(t):
        at = pl.multiple_of(t * TILE, TILE)
        source[t] = stage[:, pl.ds(at, TILE)].astype(F32).reshape(16, 128).astype(BF16)

    def wait_tiles(count, sem):
        tiles = source.at[pl.ds(0, count)]
        pltpu.make_async_copy(tiles, tiles, sem).wait()

    def to_partner(source_ref, target_ref, index):
        copy = pltpu.make_async_remote_copy(source_ref, target_ref, link.at[2 * index], link.at[2 * index + 1],
                                            device_id=other, device_id_type=MESH)
        copy.start()
        return copy


    def spread_plane(ahead, first_slot, count, per_plane, first_tile, target, sem):
        plane = lax.rem(y + ahead, 4)

        def send(base, columns):
            shift = 13 * (base - 32 * plane) + 9 * plane + 17 * core
            for x_to in columns:
                s = lax.rem(shift + 13 * x_to, 32)

                @pl.when(jnp.logical_and(s >= first_slot, s < first_slot + count))
                def _():
                    pltpu.make_async_remote_copy(source.at[first_tile + plane * per_plane + s], target.at[me], sem.at[0],
                                                 sem.at[1], device_id={"req": base + x_to}, device_id_type=MESH).start()
        serve(ahead, send)

    table_conv.wait()
    pl.loop(0, CONV, unroll=5)(compact)
    table_late.wait()
    pl.loop(CONV, CONV + LATE, unroll=5)(compact)
    pl.semaphore_wait(barrier, CHIPS)
    halo_copy = to_partner(latents_h.at[0, 3 * (1 - core)], halo, 0)
    for group in EARLY:
        for ahead in PLANES:
            spread_plane(ahead, *group, CONV_PLANE, 0, spread, spread_sem)
    for ahead in PLANES:
        spread_plane(ahead, LATE_SLOT, LATE_PLANE, LATE_PLANE, CONV - LATE_SLOT, late_spread, late_spread_sem)
    stale_keys = to_partner(kv_h.at[0, :, pl.ds(0, CH)], keys.at[pl.ds(POS, POS)], 1)
    stale_values = to_partner(kv_h.at[0, :, pl.ds(CH, CH)], values.at[pl.ds(POS, POS)], 2)

    for copy in ids:
        copy.wait()

    @pl.loop(0, CHIPS, unroll=8)
    def _(p):
        wanted[p] = bank[choice[parent[p]]]

    lat_copy.wait()
    for row in range(ROWS):
        activate(row + 1, window, latents[row], None)
    halo_copy.wait()
    activate(0, window, halo[...], core == 0)
    activate(ROWS + 1, window, halo[...], core == 1)
    base[...] = latents[...].reshape(POS, CH).astype(F32)

    def convolve(dy):
        weight_copies[dy].wait()
        base[...] += mm(window[dy * WIDTH:dy * WIDTH + POS, :], weight[dy * 3 * CH:(dy + 1) * 3 * CH, :])

    def pick_out(mine, received, chosen, tile, in_sem, sent_sem, out_sem):
        received[me] = source[mine]
        wait_tiles(CHIPS - 1, in_sem.at[1])
        adapter[tile] = received[wanted[me]]
        for ahead in PLANES:
            def send(base, columns):
                for x_to in columns:
                    chosen[base + x_to] = received[wanted[base + x_to]]
                for x_to in columns:
                    pltpu.make_async_remote_copy(chosen.at[base + x_to], adapter.at[tile], sent_sem, out_sem(ahead),
                                                 device_id={"req": base + x_to}, device_id_type=MESH).start()
            serve(ahead, send)

    def pick_conv():
        at = CONV_PLANE * y + slot
        pick_out(at, spread, picked, CONV * core + at, spread_sem, pick_sent, lambda ahead: pick_sem.at[ahead])

    pl.when(slot < EARLY[1][0])(pick_conv)
    convolve(0)
    pl.when(jnp.logical_and(holds, slot >= EARLY[1][0]))(pick_conv)

    @pl.when(holds_late)
    def _():
        at = LATE_PLANE * y + slot - LATE_SLOT
        pick_out(CONV + at, late_spread, late_picked, 2 * CONV + LATE * core + at, late_spread_sem,
                 late_pick_sem.at[0], lambda ahead: late_pick_sem.at[1])

    convolve(1)
    convolve(2)

    def wait_split(count, own, sem):
        @pl.when(own)
        def _():
            wait_tiles(count - 1, sem)

        @pl.when(jnp.logical_not(own))
        def _():
            wait_tiles(count, sem)

    forwards = []
    starts = []
    for ahead in PLANES:
        plane = lax.rem(y + 4 - ahead, 4)
        if ahead == 0:
            wait_split(CONV_PLANE, holds, pick_sem.at[ahead])
        else:
            wait_tiles(CONV_PLANE, pick_sem.at[ahead])
        at = CONV * core + CONV_PLANE * plane
        part = adapter.at[pl.ds(at, CONV_PLANE)]
        forwards.append(to_partner(part, part, 4 + ahead))
        unfold_down(adapter, at, CONV_PLANE, wide, at * 32)
        starts.append(CONV * (1 - core) + CONV_PLANE * plane)

    def low_part(part):
        if part == 0:
            got = mm(window[0:POS, :], wide[0:3 * CH, :].astype(BF16))
            return got + mm(window[WIDTH:WIDTH + POS, 0:2 * CH], wide[3 * CH:5 * CH, :].astype(BF16))
        got = mm(window[WIDTH:WIDTH + POS, 2 * CH:3 * CH], wide[5 * CH:6 * CH, :].astype(BF16))
        return got + mm(window[2 * WIDTH:2 * WIDTH + POS, :], wide[6 * CH:9 * CH, :].astype(BF16))

    @pl.when(core == 0)
    def _():
        low[...] = low_part(0)

    @pl.when(core == 1)
    def _():
        low[...] = low_part(1)

    for forward, at in zip(forwards, starts):
        forward.wait()
        unfold_down(adapter, at, CONV_PLANE, wide, at * 32)

    @pl.when(core == 0)
    def _():
        low[...] += low_part(1)

    @pl.when(core == 1)
    def _():
        low[...] += low_part(0)

    up = unfold_up(adapter, 180, tall, 0)
    hidden = (base[...] + mm(low[...][:, :RANK].astype(BF16), up)).astype(BF16)
    hidden_s[...] = hidden
    for copy in later:
        copy.wait()
    h = hidden.astype(F32)
    centred = h - jnp.mean(h, axis=-1, keepdims=True)
    var = jnp.mean(centred * centred, axis=-1, keepdims=True)
    normed = (gain[...].reshape(1, CH) * centred * lax.rsqrt(var + 1e-5)).astype(BF16)

    projected = mm(normed, wkqv[...])
    keys[0:POS, :] = projected[:, :CH].astype(BF16)
    wait_split(LATE, holds_late, late_pick_sem.at[1])
    half = adapter.at[pl.ds(2 * CONV + LATE * core, LATE)]
    late_forward = to_partner(half, half, 3)
    stale_keys.wait()
    stale_values.wait()
    late_forward.wait()
    unfold_down(adapter, 200, 20, wide, 0)
    unfold_down(adapter, 240, 20, wide, CH)
    downs = [wide[0:CH, :].astype(BF16), wide[CH:2 * CH, :].astype(BF16)]
    lows = mm(normed, jnp.concatenate(downs, axis=1)).astype(BF16)
    query[...] = (projected[:, CH:2 * CH] + mm(lows[:, :RANK], unfold_up(adapter, 220, tall, 320))).astype(BF16)
    values[0:POS, :] = (projected[:, 2 * CH:] + mm(lows[:, 128:128 + RANK], unfold_up(adapter, 260, tall, 640))).astype(BF16)

    scale = math.log2(math.e) / math.sqrt(CH // HEADS)
    block = POS // 2
    ones = jnp.ones((2 * POS, 128), BF16)
    low_lanes = lax.broadcasted_iota(jnp.int32, (block, 128), 1) < RANK

    @pl.loop(0, HEADS // 2, unroll=HEADS // 2)
    def _(pair):
        lanes = pl.ds(pl.multiple_of(pair * 128, 128), 128)
        k2 = keys[:, lanes]
        v2 = jnp.concatenate([values[:, lanes], ones], axis=1)
        for part in range(2):
            rows = pl.ds(part * block, block)
            q2 = query[rows, lanes]
            heads = []
            for side in (low_lanes, jnp.logical_not(low_lanes)):
                scores = lax.dot_general(jnp.where(side, q2, jnp.zeros_like(q2)), k2, (((1,), (1,)), ((), ())),
                                         preferred_element_type=F32)
                top = jnp.max(scores, axis=-1, keepdims=True)
                weights = jnp.exp2((scores - top) * scale).astype(BF16)
                heads.append(mm(weights, v2))
            total = jnp.where(low_lanes, heads[0][:, 128:], heads[1][:, 128:])
            mixed[rows, lanes] = (jnp.where(low_lanes, heads[0][:, :128], heads[1][:, :128]) / total).astype(BF16)

    for part in range(2):
        rows, image = pl.ds(part * block, block), pl.ds(part * (ROWS // 2), ROWS // 2)
        result = hidden_s[rows, :].astype(F32) + mm(mixed[rows, :], wo[...])
        out[0, image] = result.astype(BF16).reshape(ROWS // 2, WIDTH, CH)

    wait_split(CONV, holds, spread_sem.at[0])
    wait_split(LATE, holds_late, late_spread_sem.at[0])

    @pl.when(holds)
    def _():
        wait_tiles(CHIPS - 1, pick_sent)

    @pl.when(holds_late)
    def _():
        wait_tiles(CHIPS - 1, late_pick_sem.at[0])


def body(latents, previous_key_values, convolution_kernel_weight, layer_norm_gain, query_matrix, key_matrix,
         value_matrix, output_matrix, adapter_table, request_adapter_choice, parent_request, adapter_bank_row):
    here = pl.BlockSpec(memory_space=pltpu.HBM)
    ids = pltpu.SMEM((CHIPS,), jnp.int32)
    tiles = pltpu.VMEM((CHIPS, 16, 128), BF16)
    return pl.pallas_call(
        kernel,
        out_shape=jax.ShapeDtypeStruct(latents.shape, BF16),
        in_specs=[here] * 12,
        out_specs=pl.BlockSpec(memory_space=pltpu.VMEM),
        scratch_shapes=[
            ids, ids, ids, ids,
            pltpu.VMEM((1, (CONV + LATE) * TILE), BF16),
            pltpu.VMEM((ROWS, WIDTH, CH), BF16),
            pltpu.VMEM((9 * CH, CH), BF16),
            pltpu.VMEM((CH,), F32),
            pltpu.VMEM((CH, 3 * CH), BF16),
            pltpu.VMEM((CH, CH), BF16),
            pltpu.VMEM((CONV + LATE, 16, 128), BF16),
            tiles, tiles, tiles, tiles,
            pltpu.VMEM((2 * (CONV + LATE), 16, 128), BF16),
            pltpu.VMEM((WIDTH, CH), BF16),
            pltpu.VMEM(((ROWS + 2) * WIDTH, 3 * CH), BF16),
            pltpu.VMEM((POS, CH), F32),
            pltpu.VMEM((2 * CONV * 32, 128), F32),
            pltpu.VMEM((960, 128), F32),
            pltpu.VMEM((POS, 128), F32),
            pltpu.VMEM((POS, CH), BF16),
            pltpu.VMEM((POS, CH), BF16),
            pltpu.VMEM((2 * POS, CH), BF16),
            pltpu.VMEM((2 * POS, CH), BF16),
            pltpu.VMEM((POS, CH), BF16),
            pltpu.SemaphoreType.DMA((14,)),
            pltpu.SemaphoreType.DMA((2,)),
            pltpu.SemaphoreType.DMA,
            pltpu.SemaphoreType.DMA((4,)),
            pltpu.SemaphoreType.DMA((2,)),
            pltpu.SemaphoreType.DMA((2,)),
            pltpu.SemaphoreType.DMA((16,)),
        ],
        compiler_params=pltpu.CompilerParams(collective_id=0, has_side_effects=True, vmem_limit_bytes=44 << 20),
    )(*[pltpu.with_memory_space_constraint(a, pltpu.HBM) for a in (
        request_adapter_choice, parent_request, adapter_bank_row, adapter_table, previous_key_values, latents,
        convolution_kernel_weight, layer_norm_gain, query_matrix, key_matrix, value_matrix, output_matrix)])


def solution(mesh):
    placed = (P("req", "patch", None, None), P("req", "patch", None), P(), P(), P(), P(), P(), P(),
              P("req", None), P(), P(), P())
    return jax.shard_map(body, mesh=mesh, in_specs=placed, out_specs=P("req", "patch", None, None), check_vma=False)
```
